256 devices in a mesh: panel: 32 (over x, z), obs: 8 (over y, core).
Axes of the slice: x: 4, y: 4, z: 8, core: 2. Of those that a mesh axis runs over, the one named last changes fastest.
Arguments:
- series: float32 [256, 5, 65536], P('obs', None, 'panel'), may hold values from -6 to 6
- panel_pos: float32 [3, 65536], P(None, 'panel'), may hold values from -1 to 1
- panel_area: float32 [3, 65536], P(None, 'panel'), may hold values from -3 to 3
- observers: float32 [3, 1024], replicated, may hold values from -4 to 4, as said below
- owner: int32 [65536], P('panel'), may hold values from -1 to 31, as said below
Outputs:
- spectrum: float32 [1024, 2, 32], P('panel', None, 'obs')
The draws below stay inside these ranges and needn't reach their ends.
Inputs may be any that keep to these rules, and one draw needn't show every extreme that they name: `owner`: on each device the live slots come first and the empty ones hold -1; the number of live slots of a device is a multiple of 32, and its live slots name every device of the panel axis equally often, at most 64 times, a device with all 2048 slots live reaching that. In all, every device is named by exactly 1024 slots. `observers`: the first coordinate of every observer lies between 2 and 4, the other two between -4 and 4.
All inputs are finite; a program needn't handle non-finite values.
Results may differ from the reference program's by a relative error of at most 0.0003.
Values sent between devices are 32-bit elements; how exact they have to be, the bound alone decides.
No kernel may reach another device: no remote copies, remote signals or barrier semaphores. Data moves between devices by JAX's collectives and lax.ppermute only.
A program may use at most 64 MiB of HBM per device.

```python
import math
import jax
import jax.numpy as jnp
from jax import lax

TIME = 256
FIELDS = 5
FREQ = 32
OBSERVERS = 1024
PAN_DEV = 1024
SLOTS = 2048
SLOTS_ALL = 65536
N_PANEL = 32


def draw_owner(key, part):
    key = jax.random.fold_in(key, 11)
    share = PAN_DEV // N_PANEL
    key_perm, key_offsets, key_slots = jax.random.split(key, 3)
    shuffle = jax.random.permutation(key_perm, N_PANEL)
    offsets = jax.random.randint(key_offsets, (N_PANEL // 2,), 0, share + 1)
    offsets = offsets.at[0].set(share)
    shares = jnp.zeros((N_PANEL,), jnp.int32)
    shares = shares.at[shuffle[0::2]].set(share + offsets).at[shuffle[1::2]].set(share - offsets)
    slot_ids = jnp.arange(SLOTS, dtype=jnp.int32)

    def one_device(device, share_now):
        live_now = slot_ids < share_now * N_PANEL
        scores = jax.random.randint(jax.random.fold_in(key_slots, device), (SLOTS,), 0, 65536)
        scores = jnp.where(live_now, scores, 131072) * SLOTS + slot_ids
        ordering = jnp.argsort(scores, stable=True).astype(jnp.int32)
        return jnp.where(live_now, ordering % N_PANEL, -1)
    return jax.vmap(one_device)(jnp.arange(N_PANEL, dtype=jnp.int32), shares).reshape(-1)


def draw_observers(key, part):
    key = jax.random.fold_in(key, 5)
    uniform_now = jax.random.uniform(key, (3, OBSERVERS), jnp.float32)
    depth = 2.0 + 2.0 * uniform_now[0]
    sideways = 8.0 * uniform_now[1:3] - 4.0
    return jnp.concatenate([depth[None, :], sideways], axis=0)


def levels(stream_key, dims, cuts, low, high):
    level, own = 1.0, jax.random.fold_in(stream_key, 6)
    for dim, parts in cuts:
        draws = jnp.exp(jax.random.uniform(jax.random.fold_in(own, dim), (parts,), jnp.float32, low / len(cuts), high / len(cuts)))
        level = level * jnp.repeat(draws, dims[dim] // parts).reshape([-1 if axis == dim else 1 for axis in range(len(dims))])
    return level


def normal_values(key, dims, spread, reach, cuts=(), held_as=jnp.bfloat16):
    values = spread * jax.random.normal(key, dims, jnp.float32)
    if cuts:
        values = values * levels(key, dims, cuts, -0.22, 0.18)
    return jnp.clip(values, -reach, reach).astype(held_as)


def setup_inputs(seed: int = 0) -> dict:
    arg_keys = jax.random.split(jax.random.key(seed), 6)
    return {
        "series": normal_values(arg_keys[0], (TIME, FIELDS, SLOTS_ALL), 1.0, 6.0, ((0, 8), (2, 32)), jnp.float32),
        "panel_pos": jnp.clip(jax.random.uniform(arg_keys[1], (3, SLOTS_ALL), jnp.float32, -1.0, 1.0) * levels(arg_keys[1], (3, SLOTS_ALL), ((1, 32),), -0.4, 0.0), -1.0, 1.0),
        "panel_area": normal_values(arg_keys[2], (3, SLOTS_ALL), 0.5, 3.0, ((1, 32),), jnp.float32),
        "observers": draw_observers(jax.random.fold_in(arg_keys[5], 71), 0),
        "owner": draw_owner(jax.random.fold_in(arg_keys[5], 71), 0),
    }


PRECISE = lax.Precision.HIGHEST
MACH_NUMBER = 0.3
DENSITY = 1.0
SAMPLE_SPACING = 0.04
FOUR_PI = 4.0 * math.pi

def fourier_rows(harmonic, instant):
    turns = harmonic[:, None] * instant[None, :] % TIME
    angle = turns.astype(jnp.float32) * (2.0 * math.pi / TIME)
    return jnp.stack([jnp.cos(angle) * (2.0 / TIME), -jnp.sin(angle) * (2.0 / TIME)], axis=1)

def panel_columns(band, position, area_vec, wavenumber):
    real_part = band[0:5]
    imag_part = band[5:10]
    convect = MACH_NUMBER * area_vec[0]
    flux_real = DENSITY * (area_vec[0] * real_part[1] + area_vec[1] * real_part[2] + area_vec[2] * real_part[3]) + convect * real_part[0]
    flux_imag = DENSITY * (area_vec[0] * imag_part[1] + area_vec[1] * imag_part[2] + area_vec[2] * imag_part[3]) + convect * imag_part[0]
    mono_real = -wavenumber * flux_imag
    mono_imag = wavenumber * flux_real
    load_real = [area_vec[axis_id] * real_part[4] + DENSITY * convect * real_part[1 + axis_id] for axis_id in range(3)]
    load_imag = [area_vec[axis_id] * imag_part[4] + DENSITY * convect * imag_part[1 + axis_id] for axis_id in range(3)]
    moment_real = -(position[0] * load_real[0] + position[1] * load_real[1] + position[2] * load_real[2])
    moment_imag = -(position[0] * load_imag[0] + position[1] * load_imag[1] + position[2] * load_imag[2])
    cols_real = jnp.stack([mono_real] + load_real + [moment_real], axis=1)
    cols_imag = jnp.stack([mono_imag] + load_imag + [moment_imag], axis=1)
    return (cols_real, cols_imag)

def propagate(listener, position, cols_real, cols_imag, wavenumber):
    delta_x = listener[0][:, None] - position[0][None, :]
    delta_y = listener[1][:, None] - position[1][None, :]
    delta_z = listener[2][:, None] - position[2][None, :]
    distance = jnp.sqrt(delta_x * delta_x + delta_y * delta_y + delta_z * delta_z)
    phase_angle = wavenumber * distance
    inverse = 1.0 / (FOUR_PI * distance)
    green_real = jnp.cos(phase_angle) * inverse
    green_imag = -jnp.sin(phase_angle) * inverse
    inverse_square = 1.0 / (distance * distance)
    dipole_real = (green_real - phase_angle * green_imag) * inverse_square
    dipole_imag = (green_imag + phase_angle * green_real) * inverse_square
    lever_real = listener[0][:, None] * cols_real[:, 1][None, :] + listener[1][:, None] * cols_real[:, 2][None, :] + listener[2][:, None] * cols_real[:, 3][None, :] + cols_real[:, 4][None, :]
    lever_imag = listener[0][:, None] * cols_imag[:, 1][None, :] + listener[1][:, None] * cols_imag[:, 2][None, :] + listener[2][:, None] * cols_imag[:, 3][None, :] + cols_imag[:, 4][None, :]
    mono_real = cols_real[:, 0][None, :]
    mono_imag = cols_imag[:, 0][None, :]
    term_real = green_real * mono_real - green_imag * mono_imag + dipole_real * lever_real - dipole_imag * lever_imag
    term_imag = green_real * mono_imag + green_imag * mono_real + dipole_real * lever_imag + dipole_imag * lever_real
    return jnp.stack([lax.optimization_barrier(jnp.sum(term_real, axis=1)), lax.optimization_barrier(jnp.sum(term_imag, axis=1))], axis=1)

def reference(series, panel_pos, panel_area, observers, owner):
    live_flag = (owner >= 0).astype(jnp.float32)
    area_vec = panel_area * live_flag[None, :]
    harmonic_all = jnp.arange(1, FREQ + 1, dtype=jnp.int32)
    rows_now = fourier_rows(harmonic_all, jnp.arange(TIME, dtype=jnp.int32))
    spectra = jnp.einsum('kct,tfs->kcfs', rows_now, series, precision=PRECISE).reshape(FREQ, 2 * FIELDS, SLOTS_ALL)
    pos_blocks = jnp.transpose(panel_pos.reshape(3, N_PANEL, SLOTS), (1, 0, 2))

    def one_band(packed):
        band, harmonic = packed
        wavenumber = harmonic.astype(jnp.float32) * (2.0 * math.pi / (TIME * SAMPLE_SPACING))
        cols_real, cols_imag = panel_columns(band, panel_pos, area_vec, wavenumber)

        def add_block(running, pieces):
            block_pos, block_real, block_imag = pieces
            return (running + propagate(observers, block_pos, block_real, block_imag, wavenumber), None)
        pieces = (pos_blocks, cols_real.reshape(N_PANEL, SLOTS, 5), cols_imag.reshape(N_PANEL, SLOTS, 5))
        running, unused = lax.scan(add_block, jnp.zeros((OBSERVERS, 2), jnp.float32), pieces)
        return running
    result = lax.map(one_band, (spectra, harmonic_all))
    return jnp.transpose(result, (1, 2, 0))
```

```python
import math

import jax
import jax.numpy as jnp
import numpy as np
from jax import lax
from jax.experimental import pallas as pl
from jax.experimental.pallas import tpu as pltpu
from jax.sharding import PartitionSpec as P

TIME = 256
FREQ = 32
MACH_NUMBER = 0.3
SAMPLE_SPACING = 0.04
FOUR_PI = 4.0 * math.pi
BASE = 2.0 * math.pi / (TIME * SAMPLE_SPACING)

OBSERVERS = 1024
SLOTS = 2048
HALF = SLOTS // 2
STEPS = 32
CHIPS = 4
BAND = 8
LIST = 256
GROUP = 16
DEPTH = 128
MIB = 1 << 20

F32 = jnp.float32
BF16 = jnp.bfloat16


def sine_fits():
    node = np.cos((np.arange(400) + 0.5) * np.pi / 400) * 0.5 + 0.5
    square = node * 1.3**2
    angle = np.sqrt(square)
    table = []
    for values, degree in ((np.sin(angle) / angle, 5), (np.cos(angle), 6)):
        fit = np.polynomial.chebyshev.Chebyshev.fit(square, values, degree, domain=[0, 1.3**2])
        table.append([float(v) for v in fit.convert(kind=np.polynomial.Polynomial).coef])
    return table


SIN_FIT, COS_FIT = sine_fits()


def fourier_table():
    out = np.zeros((8, 64, 192), np.float32)
    high_out = np.zeros((8, 64, 192), np.float32)
    for block in range(8):
        chip, core = block // 2, block % 2
        for rel in range(CHIPS):
            band = (chip + rel) % CHIPS
            for part in range(2):
                for k in range(BAND):
                    row = (rel * 2 + part) * BAND + k
                    for source in range(2):
                        steps = 64 * chip + 32 * (core ^ source) + np.arange(STEPS)
                        turns = (BAND * band + k + 1) * steps % TIME
                        angle = turns * (2.0 * np.pi / TIME)
                        val = (np.cos(angle) if part == 0 else -np.sin(angle)) * (2.0 / TIME)
                        val = val.astype(np.float32)
                        high = val.astype(jnp.bfloat16).astype(np.float32)
                        low = (val - high).astype(np.float32)
                        lane = 32 * source
                        high_out[block, row, lane : lane + 32] = high
                        high_out[block, row, 64 + lane : 96 + lane] = high
                        high_out[block, row, 128 + lane : 160 + lane] = low
    return high_out.astype(jnp.bfloat16)


def params():
    return pltpu.CompilerParams(vmem_limit_bytes=56 * MIB)


def split(value):
    high = value.astype(BF16)
    low = (value - high.astype(F32)).astype(BF16)
    return high, low


def source_kernel(series_ref, area_ref, owner_ref, keep_ref, send_ref):
    core = lax.rem(lax.axis_index("obs"), 2)
    live = (owner_ref[...] >= 0).astype(F32)
    area = area_ref[...] * live
    a1, a2, a3 = area[0:1], area[1:2], area[2:3]
    convect = MACH_NUMBER * a1
    for pair in range(8):
        blocks = []
        for side in range(2):
            lanes = slice(128 * (2 * pair + side), 128 * (2 * pair + side) + 128)
            field = [series_ref[:, f, lanes] for f in range(5)]
            b1, b2, b3, bc = a1[:, lanes], a2[:, lanes], a3[:, lanes], convect[:, lanes]
            flux = b1 * field[1] + b2 * field[2] + b3 * field[3] + bc * field[0]
            blocks.append(
                [
                    flux,
                    b1 * field[4] + bc * field[1],
                    b2 * field[4] + bc * field[2],
                    b3 * field[4] + bc * field[3],
                ]
            )
        lanes = slice(128 * pair, 128 * pair + 128)
        for f in range(4):
            even, odd = blocks[0][f], blocks[1][f]
            rows = slice(32 * f, 32 * f + 32)
            keep_ref[rows, lanes] = jnp.where(core == 0, even, odd)
            send_ref[rows, lanes] = jnp.where(core == 0, odd, even)


def band_kernel(keep_ref, recv_ref, table_ref, own_ref, up_ref, down_ref, far_a_ref, far_b_ref):
    table = table_ref[lax.axis_index("obs")]
    for f in range(4):
        rows = slice(32 * f, 32 * f + 32)
        for tile in range(HALF // 256):
            lanes = slice(256 * tile, 256 * tile + 256)
            kh, kl = split(keep_ref[rows, lanes])
            rh, rl = split(recv_ref[rows, lanes])
            stack = jnp.concatenate([kh, rh, kl, rl, kh, rh], axis=0)
            part = jnp.dot(table, stack, preferred_element_type=F32)
            out = slice(HALF * f + 256 * tile, HALF * f + 256 * tile + 256)
            own_ref[:, out] = part[0:16]
            up_ref[:, out] = part[16:32]
            down_ref[:, out] = part[48:64]
            if f < 2:
                far_a_ref[:, out] = part[32:48]
            else:
                half = slice(out.start - 2 * HALF, out.stop - 2 * HALF)
                far_b_ref[:, half] = part[32:48]


def double(cosine, sine):
    twice = cosine + cosine
    return twice * cosine - 1.0, twice * sine


def geometry_kernel(pos_ref, obs_ref, r_ref, er_ref, ei_ref, gr_ref, gi_ref):
    place = lax.axis_index("obs")
    core = lax.rem(place, 2)
    chip = lax.div(place, 2)
    pos = jnp.where(core == 0, pos_ref[:, 0:128], pos_ref[:, 128:256])
    pos = jnp.concatenate([pos, jnp.zeros((5, 128), F32)], axis=0)
    pos = jnp.transpose(pos)

    def body(power):
        for g in range(16):
            rows = slice(8 * g, 8 * g + 8)
            y = [jnp.broadcast_to(pos[rows, i : i + 1], (8, 128)) for i in range(3)]
            for tile in range(LIST // 128):
                lanes = slice(128 * tile, 128 * tile + 128)
                square = None
                for i in range(3):
                    delta = obs_ref[i : i + 1, lanes] - y[i]
                    square = delta * delta if square is None else square + delta * delta
                inverse = lax.rsqrt(square)
                r = square * inverse
                half = r * (0.5 * BASE) - 0.5 * math.pi
                s2 = half * half
                sine = jnp.full_like(s2, SIN_FIT[-1])
                for c in SIN_FIT[-2::-1]:
                    sine = sine * s2 + c
                sine = sine * half
                cosine = jnp.full_like(s2, COS_FIT[-1])
                for c in COS_FIT[-2::-1]:
                    cosine = cosine * s2 + c
                twice = sine + sine
                er = twice * sine - 1.0
                ei = twice * cosine
                amp = inverse * inverse * inverse * (1.0 / FOUR_PI)
                if power == 0:
                    gr, gi = amp, jnp.zeros_like(amp)
                else:
                    cr, ci = er, ei
                    for _ in range(3):
                        cr, ci = double(cr, ci)
                    if power == 2:
                        cr, ci = double(cr, ci)
                    elif power == 3:
                        dr, di = double(cr, ci)
                        cr, ci = cr * dr - ci * di, cr * di + ci * dr
                    gr, gi = amp * cr, amp * ci
                r_ref[rows, lanes] = r
                er_ref[rows, lanes] = er
                ei_ref[rows, lanes] = ei
                gr_ref[rows, lanes] = gr
                gi_ref[rows, lanes] = gi

    for power in range(CHIPS):
        pl.when(chip == power)(lambda power=power: body(power))


def build_left(spec, pos_ref, wave_ref, stage, left):
    core = lax.rem(lax.axis_index("obs"), 2)
    first_band = lax.div(lax.axis_index("obs"), 2) * BAND
    wave = (lax.broadcasted_iota(jnp.int32, (BAND, 128), 0) + (first_band + 1)).astype(F32) * BASE
    left[...] = jnp.zeros(left.shape, BF16)

    def chunk(c, carry):
        lanes = pl.ds(pl.multiple_of(c * 128, 128), 128)
        wide = pl.multiple_of(c * 256, 256)
        y = jnp.where(
            core == 0, pos_ref[:, pl.ds(wide, 128)], pos_ref[:, pl.ds(wide + 128, 128)]
        )
        y = [y[i : i + 1] for i in range(3)]
        square = y[0] * y[0] + y[1] * y[1] + y[2] * y[2]
        flux = spec(0, c)
        load = [spec(1 + i, c) for i in range(3)]
        gains = (-wave * flux[1], wave * flux[0])
        moment = [
            -(y[0] * load[0][p] + y[1] * load[1][p] + y[2] * load[2][p]) for p in range(2)
        ]
        for p in range(2):
            g = gains[p]
            rows = [gains[p] * square + moment[p]]
            rows += [load[i][p] - 2.0 * (y[i] * g) for i in range(3)]
            rows += [g]
            for q in range(5):
                stage[p, 8 * q : 8 * q + 8, :] = rows[q]
            rows = [wave * moment[p]] + [wave * load[i][p] for i in range(3)]
            for q in range(4):
                stage[2 + p, 8 * q : 8 * q + 8, :] = rows[q]
            stage[2 + p, 32:40, :] = jnp.zeros((8, 128), F32)
        for comp in range(4):
            for k in range(BAND):
                rows = stage[comp, pl.ds(k, 8, stride=8), :]
                rows = jnp.concatenate(
                    [rows, jnp.zeros((120, 128), F32)], axis=0
                )
                turned = jnp.transpose(rows)[:, 0:8]
                high, low = split(turned)
                block = jnp.concatenate([high, low, high], axis=1).reshape(8, GROUP, 24)
                left[pl.ds(c * 8, 8), k * 4 + comp, :, 0:24] = block
        return carry

    lax.fori_loop(0, HALF // 128, chunk, 0)


def field_kernel(
    own_ref, up_ref, down_ref, pos_ref, feature_ref,
    r_ref, er_ref, ei_ref, gr_ref, gi_ref,
    out_ref, stage, left, result, total,
):
    tile, quarter = pl.program_id(0), pl.program_id(1)

    def spec(f, c):
        lanes = pl.ds(pl.multiple_of(HALF * f + c * 128, 128), 128)
        value = own_ref[:, lanes] + up_ref[:, lanes] + down_ref[:, lanes]
        return value[0:8], value[8:16]

    @pl.when(jnp.logical_and(tile == 0, quarter == 0))
    def _():
        stage[...] = jnp.zeros(stage.shape, F32)
        build_left(spec, pos_ref, None, stage, left)

    @pl.when(quarter == 0)
    def _():
        total[...] = jnp.zeros(total.shape, F32)

    groups = 16
    first = quarter * groups

    def product(g):
        lhs = left[g].reshape(32 * GROUP, DEPTH)
        return jnp.dot(lhs, feature_ref[...], preferred_element_type=F32)

    result[0] = product(first)

    def step(g, acc):
        now = lax.rem(g, 2)

        result[1 - now] = product(first + jnp.minimum(g + 1, groups - 1))
        acc = list(acc)
        for sub in range(2):
            rows = pl.ds(pl.multiple_of(g * GROUP + 8 * sub, 8), 8)
            for lane in range(2):
                lanes = slice(128 * lane, 128 * lane + 128)
                r = r_ref[rows, lanes]
                er, ei = er_ref[rows, lanes], ei_ref[rows, lanes]
                pr, pi = gr_ref[rows, lanes], gi_ref[rows, lanes]
                cr, ci = pr * er - pi * ei, pr * ei + pi * er
                twice = er + er
                for k in range(BAND):
                    base = k * 4 * GROUP + 8 * sub
                    m = [result[now, base + GROUP * c : base + GROUP * c + 8, lanes] for c in range(4)]
                    tr = m[0] - r * m[3]
                    ti = m[1] + r * m[2]
                    slot = lane * 16 + 2 * k
                    acc[slot] = acc[slot] + (cr * tr - ci * ti)
                    acc[slot + 1] = acc[slot + 1] + (cr * ti + ci * tr)
                    if k + 1 < BAND:
                        pr, pi, cr, ci = cr, ci, twice * cr - pr, twice * ci - pi
        return tuple(acc)

    zero = jnp.zeros((8, 128), F32)
    acc = lax.fori_loop(0, groups, step, (zero,) * 32)
    for i in range(32):
        total[i] = total[i] + acc[i]

    @pl.when(quarter == 3)
    def _():
        lane_block = lax.broadcasted_iota(jnp.int32, (4, 128), 1) // 32
        for lane in range(2):
            sums = [jnp.sum(total[lane * 16 + i], axis=0, keepdims=True) for i in range(16)]
            packs = [
                jnp.concatenate(
                    [sums[2 * kk], sums[2 * kk + 1], sums[2 * (4 + kk)], sums[2 * (4 + kk) + 1]],
                    axis=0,
                )
                for kk in range(4)
            ]
            for m in range(4):
                value = None
                for kk in range(4):
                    shift = (32 * (kk - m)) % 128
                    turned = pltpu.roll(packs[kk], shift, axis=1) if shift else packs[kk]
                    value = turned if value is None else jnp.where(lane_block == kk, turned, value)
                out_ref[4 * lane + m] = value


def finish_kernel(parts_ref, own_ref, send_ref):
    core = lax.rem(lax.axis_index("obs"), 2)
    value = jnp.sum(parts_ref[...], axis=0)
    own_ref[...] = jnp.where(core == 0, value[0:2], value[2:4])
    send_ref[...] = jnp.where(core == 0, value[2:4], value[0:2])


def shape(*dims, dtype=F32):
    return jax.ShapeDtypeStruct(dims, dtype)


def feature_kernel(observers_ref, out_ref):
    x = observers_ref[...]
    rows = jnp.concatenate(
        [
            jnp.ones((1, OBSERVERS), F32),
            x,
            x[0:1] * x[0:1] + x[1:2] * x[1:2] + x[2:3] * x[2:3],
            jnp.zeros((3, OBSERVERS), F32),
        ],
        axis=0,
    )
    high = rows.astype(BF16).astype(F32)
    low = rows - high
    rest = jnp.zeros((DEPTH - 24, OBSERVERS), F32)
    out_ref[...] = jnp.concatenate([high, high, low, rest], axis=0).astype(BF16)


def on_device(series, panel_pos, panel_area, observers, owner):
    whole = pl.BlockSpec(memory_space=pltpu.VMEM)
    keep, send = pl.pallas_call(
        source_kernel,
        out_shape=(shape(128, HALF), shape(128, HALF)),
        in_specs=[whole] * 3,
        out_specs=(whole, whole),
        compiler_params=params(),
        name="sources",
    )(series, panel_area, owner.reshape(1, SLOTS))
    swap = [(i, i ^ 1) for i in range(8)]
    above = [(i, (i + 2) % 8) for i in range(8)]
    below = [(i, (i + 6) % 8) for i in range(8)]
    recv = lax.ppermute(send, "obs", swap)

    pair_count = HALF * OBSERVERS
    block = pl.BlockSpec((128, LIST), lambda i, j: (i, j))
    geometry = pl.pallas_call(
        geometry_kernel,
        grid=(HALF // 128, OBSERVERS // LIST),
        out_shape=(shape(HALF, OBSERVERS),) * 5,
        in_specs=[
            pl.BlockSpec((3, 256), lambda i, j: (0, i)),
            pl.BlockSpec((3, LIST), lambda i, j: (0, j)),
        ],
        out_specs=(block,) * 5,
        compiler_params=params(),
        cost_estimate=pl.CostEstimate(
            flops=80 * pair_count, bytes_accessed=20 * pair_count, transcendentals=pair_count
        ),
        name="geometry",
    )(panel_pos, observers)

    own, up, down, far_a, far_b = pl.pallas_call(
        band_kernel,
        out_shape=(shape(16, 4 * HALF),) * 3 + (shape(16, 2 * HALF),) * 2,
        in_specs=[whole] * 3,
        out_specs=(whole,) * 5,
        compiler_params=params(),
        name="bands",
    )(keep, recv, jnp.asarray(fourier_table()))

    got_a = lax.ppermute(far_a, "obs", above)
    got_b = lax.ppermute(far_b, "obs", below)
    pad = jnp.zeros((16, 2 * HALF), F32)
    up = up + jnp.concatenate([got_a, pad], axis=1)
    down = down + jnp.concatenate([pad, got_b], axis=1)
    from_below = lax.ppermute(up, "obs", above)
    from_above = lax.ppermute(down, "obs", below)

    features = pl.pallas_call(
        feature_kernel,
        out_shape=shape(DEPTH, OBSERVERS, dtype=BF16),
        in_specs=[whole],
        out_specs=whole,
        compiler_params=params(),
        name="features",
    )(observers)
    quarter = HALF // 4
    near = pl.BlockSpec((quarter, LIST), lambda t, q: (q, t))
    chunks = pl.pallas_call(
        field_kernel,
        grid=(OBSERVERS // LIST, 4),
        out_shape=shape(32, 4, 128),
        in_specs=[whole] * 4 + [pl.BlockSpec((DEPTH, LIST), lambda t, q: (0, t))] + [near] * 5,
        out_specs=pl.BlockSpec((8, 4, 128), lambda t, q: (t, 0, 0)),
        scratch_shapes=[
            pltpu.VMEM((4, 64, 128), F32),
            pltpu.VMEM((HALF // GROUP, 32, GROUP, DEPTH), BF16),
            pltpu.VMEM((2, 32 * GROUP, LIST), F32),
            pltpu.VMEM((32, 8, 128), F32),
        ],
        compiler_params=params(),
        name="field",
    )(own, from_below, from_above, panel_pos, features, *geometry)

    parts = lax.all_to_all(chunks, "panel", split_axis=0, concat_axis=0, tiled=True)
    mine, other = pl.pallas_call(
        finish_kernel,
        out_shape=(shape(2, 128), shape(2, 128)),
        in_specs=[whole],
        out_specs=(whole, whole),
        compiler_params=params(),
        name="finish",
    )(parts)
    value = mine + lax.ppermute(other, "obs", swap)
    return jnp.transpose(value.reshape(2, 4, 32), (2, 0, 1))


def solution(mesh):
    in_specs = (P("obs", None, "panel"), P(None, "panel"), P(None, "panel"), P(), P("panel"))
    out_specs = P("panel", None, "obs")
    return jax.shard_map(
        on_device, mesh=mesh, in_specs=in_specs, out_specs=out_specs, check_vma=False
    )
```

```python
import math

import jax
import jax.numpy as jnp
import numpy as np
from jax import lax
from jax.experimental import pallas as pl
from jax.experimental.pallas import tpu as pltpu
from jax.sharding import PartitionSpec as P

TIME = 256
FREQ = 32
MACH_NUMBER = 0.3
SAMPLE_SPACING = 0.04
FOUR_PI = 4.0 * math.pi
BASE = 2.0 * math.pi / (TIME * SAMPLE_SPACING)

OBSERVERS = 1024
SLOTS = 2048
HALF = SLOTS // 2
STEPS = 32
CHIPS = 4
BAND = 8
LIST = 256
GROUP = 16
BATCH = 128
PIECES = 8
DEPTH = 128
MIB = 1 << 20

F32 = jnp.float32
BF16 = jnp.bfloat16


def sine_fits():
    node = np.cos((np.arange(400) + 0.5) * np.pi / 400) * 0.5 + 0.5
    square = node * 1.3**2
    angle = np.sqrt(square)
    table = []
    for values, degree in ((np.sin(angle) / angle, 5), (np.cos(angle), 6)):
        fit = np.polynomial.chebyshev.Chebyshev.fit(square, values, degree, domain=[0, 1.3**2])
        table.append([float(v) for v in fit.convert(kind=np.polynomial.Polynomial).coef])
    return table


SIN_FIT, COS_FIT = sine_fits()


def fourier_table():
    out = np.zeros((8, 64, 192), np.float32)
    high_out = np.zeros((8, 64, 192), np.float32)
    for block in range(8):
        chip, core = block // 2, block % 2
        for rel in range(CHIPS):
            band = (chip + rel) % CHIPS
            for part in range(2):
                for k in range(BAND):
                    row = (rel * 2 + part) * BAND + k
                    for source in range(2):
                        steps = 64 * chip + 32 * (core ^ source) + np.arange(STEPS)
                        turns = (BAND * band + k + 1) * steps % TIME
                        angle = turns * (2.0 * np.pi / TIME)
                        val = (np.cos(angle) if part == 0 else -np.sin(angle)) * (2.0 / TIME)
                        val = val.astype(np.float32)
                        high = val.astype(jnp.bfloat16).astype(np.float32)
                        low = (val - high).astype(np.float32)
                        lane = 32 * source
                        high_out[block, row, lane : lane + 32] = high
                        high_out[block, row, 64 + lane : 96 + lane] = high
                        high_out[block, row, 128 + lane : 160 + lane] = low
    return high_out.astype(jnp.bfloat16)


def params(mib=16):
    return pltpu.CompilerParams(vmem_limit_bytes=mib * MIB)


def split(value):
    high = value.astype(BF16)
    low = (value - high.astype(F32)).astype(BF16)
    return high, low


def source_kernel(series_ref, area_ref, owner_ref, keep_ref, send_ref):
    core = lax.rem(lax.axis_index("obs"), 2)
    live = (owner_ref[...] >= 0).astype(F32)
    area = area_ref[...] * live
    blocks = []
    for side in range(2):
        lanes = slice(128 * side, 128 * side + 128)
        field = [series_ref[:, f, lanes] for f in range(5)]
        b1, b2, b3 = area[0:1, lanes], area[1:2, lanes], area[2:3, lanes]
        bc = MACH_NUMBER * b1
        flux = b1 * field[1] + b2 * field[2] + b3 * field[3] + bc * field[0]
        blocks.append([flux] + [b * field[4] + bc * field[1 + i] for i, b in enumerate((b1, b2, b3))])
    for f in range(4):
        even, odd = blocks[0][f], blocks[1][f]
        rows = slice(32 * f, 32 * f + 32)
        keep_ref[rows, :] = jnp.where(core == 0, even, odd)
        send_ref[rows, :] = jnp.where(core == 0, odd, even)


def band_kernel(keep_ref, recv_ref, table_ref, own_ref, up_ref, down_ref, far_a_ref, far_b_ref):
    table = table_ref[lax.axis_index("obs")]
    for f in range(4):
        rows = slice(32 * f, 32 * f + 32)
        for tile in range(HALF // 256):
            lanes = slice(256 * tile, 256 * tile + 256)
            kh, kl = split(keep_ref[rows, lanes])
            rh, rl = split(recv_ref[rows, lanes])
            stack = jnp.concatenate([kh, rh, kl, rl, kh, rh], axis=0)
            part = jnp.dot(table, stack, preferred_element_type=F32)
            out = slice(HALF * f + 256 * tile, HALF * f + 256 * tile + 256)
            own_ref[:, out] = part[0:16]
            up_ref[:, out] = part[16:32]
            down_ref[:, out] = part[48:64]
            if f < 2:
                far_a_ref[:, out] = part[32:48]
            else:
                half = slice(out.start - 2 * HALF, out.stop - 2 * HALF)
                far_b_ref[:, half] = part[32:48]


def double(cosine, sine):
    twice = cosine + cosine
    return twice * cosine - 1.0, twice * sine


def geometry_kernel(pos_ref, obs_ref, r_ref, er_ref, ei_ref, gr_ref, gi_ref):
    place = lax.axis_index("obs")
    core = lax.rem(place, 2)
    chip = lax.div(place, 2)

    def tile_step(power, y, first, t):
        lanes = pl.ds(pl.multiple_of(t * 128, 128), 128)
        x = [jnp.broadcast_to(obs_ref[i : i + 1, lanes], (8, 128)) for i in range(3)]
        for g in range(16):
            rows = pl.ds(pl.multiple_of(first + 8 * g, 8), 8)
            square = None
            for i in range(3):
                delta = x[i] - jnp.broadcast_to(y[8 * g : 8 * g + 8, i : i + 1], (8, 128))
                square = delta * delta if square is None else square + delta * delta
            inverse = lax.rsqrt(square)
            r = square * inverse
            half = r * (0.5 * BASE) - 0.5 * math.pi
            s2 = half * half
            sine = s2 * SIN_FIT[-1] + SIN_FIT[-2]
            for c in SIN_FIT[-3::-1]:
                sine = sine * s2 + c
            sine = sine * half
            cosine = s2 * COS_FIT[-1] + COS_FIT[-2]
            for c in COS_FIT[-3::-1]:
                cosine = cosine * s2 + c
            twice = sine + sine
            er = twice * sine - 1.0
            ei = twice * cosine
            amp = inverse * inverse * (inverse * (1.0 / FOUR_PI))
            if power == 0:
                gr, gi = amp, jnp.zeros_like(amp)
            else:
                cr, ci = er, ei
                for _ in range(3):
                    cr, ci = double(cr, ci)
                if power == 2:
                    cr, ci = double(cr, ci)
                elif power == 3:
                    dr, di = double(cr, ci)
                    cr, ci = cr * dr - ci * di, cr * di + ci * dr
                gr, gi = amp * cr, amp * ci
            r_ref[rows, lanes] = r
            er_ref[rows, lanes] = er
            ei_ref[rows, lanes] = ei
            gr_ref[rows, lanes] = gr
            gi_ref[rows, lanes] = gi

    def body(power):
        def chunk(c, carry):
            wide = pl.multiple_of(c * 256, 256)
            pos = jnp.where(
                core == 0, pos_ref[:, pl.ds(wide, 128)], pos_ref[:, pl.ds(wide + 128, 128)]
            )
            pos = jnp.concatenate([pos, jnp.zeros((5, 128), F32)], axis=0)
            y = jnp.transpose(pos)

            def tile(t, inner):
                tile_step(power, y, c * 128, t)
                return inner

            lax.fori_loop(0, OBSERVERS // 128, tile, 0)
            return carry

        lax.fori_loop(0, HALF // 128, chunk, 0)

    for power in range(CHIPS):
        pl.when(chip == power)(lambda power=power: body(power))


def build_left(spec, pos_ref, stage, left):
    core = lax.rem(lax.axis_index("obs"), 2)
    first_band = lax.div(lax.axis_index("obs"), 2) * BAND
    wave = (lax.broadcasted_iota(jnp.int32, (BAND, 128), 0) + (first_band + 1)).astype(F32) * BASE
    freq_of = lax.broadcasted_iota(jnp.int32, (128, 128), 1) // 16
    stage[...] = jnp.zeros(stage.shape, F32)

    def chunk(c, carry):
        wide = pl.multiple_of(c * 256, 256)
        y = jnp.where(
            core == 0, pos_ref[:, pl.ds(wide, 128)], pos_ref[:, pl.ds(wide + 128, 128)]
        )
        y = [y[i : i + 1] for i in range(3)]
        square = y[0] * y[0] + y[1] * y[1] + y[2] * y[2]
        flux = spec(0, c)
        load = [spec(1 + i, c) for i in range(3)]
        gains = (-wave * flux[1], wave * flux[0])
        moment = [
            -(y[0] * load[0][p] + y[1] * load[1][p] + y[2] * load[2][p]) for p in range(2)
        ]
        comps = []
        for p in range(2):
            g = gains[p]
            rows = [g * square + moment[p]]
            rows += [load[i][p] - 2.0 * (y[i] * g) for i in range(3)]
            comps.append(rows + [g])
        for p in range(2):
            comps.append([wave * moment[p]] + [wave * load[i][p] for i in range(3)])
        for comp, rows in enumerate(comps):
            for q, row in enumerate(rows):
                high = row.astype(BF16).astype(F32)
                for place, value in ((q, high), (5 + q, row - high), (10 + q, high)):
                    stage[pl.ds(128 * comp + place, 8, stride=16), :] = value
        for comp in range(4):
            turned = jnp.transpose(stage[128 * comp : 128 * comp + 128, :])
            for k in range(BAND):
                block = jnp.where(freq_of == k, turned, 0.0).astype(BF16)
                left[pl.ds(c * 8, 8), comp * BAND + k] = block.reshape(8, GROUP, DEPTH)
        return carry

    lax.fori_loop(0, HALF // 128, chunk, 0)


def field_kernel(
    own_ref, up_ref, down_ref, pos_ref, feature_ref,
    r_ref, er_ref, ei_ref, gr_ref, gi_ref,
    out_ref, stage, left, ready, after, total,
):
    def spec(f, c):
        lanes = pl.ds(pl.multiple_of(HALF * f + c * 128, 128), 128)
        value = own_ref[:, lanes] + up_ref[:, lanes] + down_ref[:, lanes]
        return value[0:8], value[8:16]

    build_left(spec, pos_ref, stage, left)
    total[...] = jnp.zeros(total.shape, F32)
    batches = HALF // BATCH
    steps = batches * (OBSERVERS // LIST)
    groups = BATCH // GROUP

    def product(target, i, part):
        t, b = lax.div(i, batches), lax.rem(i, batches)
        size = 32 * GROUP * groups // PIECES
        if PIECES <= groups:
            lhs = left[pl.ds(b * groups + part * (groups // PIECES), groups // PIECES)]
        else:
            cut = PIECES // groups
            span = 32 // cut
            lhs = left[b * groups + part // cut, span * (part % cut) : span * (part % cut) + span]
        rhs = feature_ref[:, pl.ds(pl.multiple_of(t * LIST, LIST), LIST)]
        target[part * size : part * size + size] = jnp.dot(
            lhs.reshape(size, DEPTH), rhs, preferred_element_type=F32
        )

    def consume(source, i, target, following):
        t, b = lax.div(i, batches), lax.rem(i, batches)
        for lane in range(LIST // 128):
            lanes = pl.ds(pl.multiple_of(t * LIST + 128 * lane, 128), 128)
            near = slice(128 * lane, 128 * lane + 128)
            acc = [total[t, lane * 16 + i] for i in range(16)]
            for sub in range(BATCH // 8):
                piece, rest = divmod((lane * (BATCH // 8) + sub) * PIECES, BATCH // 4)
                if rest == 0:
                    product(target, following, piece)
                rows = pl.ds(pl.multiple_of(b * BATCH + 8 * sub, 8), 8)
                r = r_ref[rows, lanes]
                er, ei = er_ref[rows, lanes], ei_ref[rows, lanes]
                pr, pi = gr_ref[rows, lanes], gi_ref[rows, lanes]
                cr, ci = pr * er - pi * ei, pr * ei + pi * er
                twice = er + er
                for k in range(BAND):
                    m = []
                    for comp in range(4):
                        base = ((sub // 2) * 32 + comp * BAND + k) * GROUP + 8 * (sub % 2)
                        m.append(source[base : base + 8, near])
                    tr = m[0] - r * m[3]
                    ti = m[1] + r * m[2]
                    acc[2 * k] = acc[2 * k] + (cr * tr - ci * ti)
                    acc[2 * k + 1] = acc[2 * k + 1] + (cr * ti + ci * tr)
                    if k + 1 < BAND:
                        pr, pi, cr, ci = cr, ci, twice * cr - pr, twice * ci - pi
            for i in range(16):
                total[t, lane * 16 + i] = acc[i]

    for part in range(PIECES):
        product(ready, 0, part)

    def step(i, carry):
        following = jnp.minimum(i + 1, steps - 1)

        @pl.when(lax.rem(i, 2) == 0)
        def _():
            consume(ready, i, after, following)

        @pl.when(lax.rem(i, 2) == 1)
        def _():
            consume(after, i, ready, following)

        return carry

    lax.fori_loop(0, steps, step, 0)

    lane_block = lax.broadcasted_iota(jnp.int32, (4, 128), 1) // 32
    for t in range(OBSERVERS // LIST):
        for lane in range(LIST // 128):
            sums = [jnp.sum(total[t, lane * 16 + i], axis=0, keepdims=True) for i in range(16)]
            packs = [
                jnp.concatenate(
                    [sums[2 * kk], sums[2 * kk + 1], sums[2 * (4 + kk)], sums[2 * (4 + kk) + 1]],
                    axis=0,
                )
                for kk in range(4)
            ]
            for m in range(4):
                value = None
                for kk in range(4):
                    shift = (32 * (kk - m)) % 128
                    turned = pltpu.roll(packs[kk], shift, axis=1) if shift else packs[kk]
                    value = turned if value is None else jnp.where(lane_block == kk, turned, value)
                out_ref[8 * t + 4 * lane + m] = value


def finish_kernel(parts_ref, own_ref, send_ref):
    core = lax.rem(lax.axis_index("obs"), 2)
    value = jnp.sum(parts_ref[...], axis=0)
    own_ref[...] = jnp.where(core == 0, value[0:2], value[2:4])
    send_ref[...] = jnp.where(core == 0, value[2:4], value[0:2])


def shape(*dims, dtype=F32):
    return jax.ShapeDtypeStruct(dims, dtype)


def feature_kernel(observers_ref, out_ref):
    x = observers_ref[...]
    rows = jnp.concatenate(
        [
            jnp.ones((1, OBSERVERS), F32),
            x,
            x[0:1] * x[0:1] + x[1:2] * x[1:2] + x[2:3] * x[2:3],
        ],
        axis=0,
    )
    high = rows.astype(BF16).astype(F32)
    low = rows - high
    rest = jnp.zeros((1, OBSERVERS), F32)
    out_ref[...] = jnp.concatenate([high, high, low, rest] * BAND, axis=0).astype(BF16)


def on_device(series, panel_pos, panel_area, observers, owner):
    whole = pl.BlockSpec(memory_space=pltpu.VMEM)
    pair = pl.BlockSpec((128, 128), lambda i: (0, i))
    keep, send = pl.pallas_call(
        source_kernel,
        grid=(HALF // 128,),
        out_shape=(shape(128, HALF), shape(128, HALF)),
        in_specs=[
            pl.BlockSpec((STEPS, 5, 256), lambda i: (0, 0, i)),
            pl.BlockSpec((3, 256), lambda i: (0, i)),
            pl.BlockSpec((1, 256), lambda i: (0, i)),
        ],
        out_specs=(pair, pair),
        compiler_params=params(),
        name="sources",
    )(series, panel_area, owner.reshape(1, SLOTS))
    swap = [(i, i ^ 1) for i in range(8)]
    above = [(i, (i + 2) % 8) for i in range(8)]
    below = [(i, (i + 6) % 8) for i in range(8)]
    recv = lax.ppermute(send, "obs", swap)

    pair_count = HALF * OBSERVERS
    geometry = pl.pallas_call(
        geometry_kernel,
        out_shape=(shape(HALF, OBSERVERS),) * 5,
        in_specs=[whole] * 2,
        out_specs=(whole,) * 5,
        compiler_params=params(),
        cost_estimate=pl.CostEstimate(
            flops=80 * pair_count, bytes_accessed=20 * pair_count, transcendentals=pair_count
        ),
        name="geometry",
    )(panel_pos, observers)

    own, up, down, far_a, far_b = pl.pallas_call(
        band_kernel,
        out_shape=(shape(16, 4 * HALF),) * 3 + (shape(16, 2 * HALF),) * 2,
        in_specs=[whole] * 3,
        out_specs=(whole,) * 5,
        compiler_params=params(),
        name="bands",
    )(keep, recv, jnp.asarray(fourier_table()))

    got_a = lax.ppermute(far_a, "obs", above)
    got_b = lax.ppermute(far_b, "obs", below)
    pad = jnp.zeros((16, 2 * HALF), F32)
    up = up + jnp.concatenate([got_a, pad], axis=1)
    down = down + jnp.concatenate([pad, got_b], axis=1)
    from_below = lax.ppermute(up, "obs", above)
    from_above = lax.ppermute(down, "obs", below)

    features = pl.pallas_call(
        feature_kernel,
        out_shape=shape(DEPTH, OBSERVERS, dtype=BF16),
        in_specs=[whole],
        out_specs=whole,
        compiler_params=params(),
        name="features",
    )(observers)
    chunks = pl.pallas_call(
        field_kernel,
        out_shape=shape(32, 4, 128),
        in_specs=[whole] * 10,
        out_specs=whole,
        scratch_shapes=[
            pltpu.VMEM((512, 128), F32),
            pltpu.VMEM((HALF // GROUP, 32, GROUP, DEPTH), BF16),
            pltpu.VMEM((32 * BATCH, LIST), F32),
            pltpu.VMEM((32 * BATCH, LIST), F32),
            pltpu.VMEM((OBSERVERS // LIST, 32, 8, 128), F32),
        ],
        compiler_params=params(24),
        name="field",
    )(own, from_below, from_above, panel_pos, features, *geometry)

    parts = lax.all_to_all(chunks, "panel", split_axis=0, concat_axis=0, tiled=True)
    mine, other = pl.pallas_call(
        finish_kernel,
        out_shape=(shape(2, 128), shape(2, 128)),
        in_specs=[whole],
        out_specs=(whole, whole),
        compiler_params=params(),
        name="finish",
    )(parts)
    value = mine + lax.ppermute(other, "obs", swap)
    return jnp.transpose(value.reshape(2, 4, 32), (2, 0, 1))


def solution(mesh):
    in_specs = (P("obs", None, "panel"), P(None, "panel"), P(None, "panel"), P(), P("panel"))
    out_specs = P("panel", None, "obs")
    return jax.shard_map(
        on_device, mesh=mesh, in_specs=in_specs, out_specs=out_specs, check_vma=False
    )
```

```python
import functools
import math

import jax
import jax.numpy as jnp
import numpy as np
from jax import lax
from jax.experimental import pallas as pl
from jax.experimental.pallas import tpu as pltpu
from jax.sharding import PartitionSpec as P

TIME = 256
FREQ = 32
MACH_NUMBER = 0.3
SAMPLE_SPACING = 0.04
FOUR_PI = 4.0 * math.pi
BASE = 2.0 * math.pi / (TIME * SAMPLE_SPACING)

OBSERVERS = 1024
SLOTS = 2048
HALF = SLOTS // 2
STEPS = 32
CHIPS = 4
BAND = 8
LIST = 256
GROUP = 16
BATCH = 256
PIECES = 16
DEPTH = 128
MIB = 1 << 20

F32 = jnp.float32
BF16 = jnp.bfloat16


def sine_fits():
    node = np.cos((np.arange(400) + 0.5) * np.pi / 400) * 0.5 + 0.5
    square = node * 1.3**2
    angle = np.sqrt(square)
    table = []
    for values, degree in ((np.sin(angle) / angle, 5), (np.cos(angle), 6)):
        fit = np.polynomial.chebyshev.Chebyshev.fit(square, values, degree, domain=[0, 1.3**2])
        table.append([float(v) for v in fit.convert(kind=np.polynomial.Polynomial).coef])
    return table


SIN_FIT, COS_FIT = sine_fits()


def fourier_rows():
    place = lax.axis_index("obs")
    chip, core = lax.div(place, 2), lax.rem(place, 2)
    row = lax.broadcasted_iota(jnp.int32, (64, 64), 0)
    lane = lax.broadcasted_iota(jnp.int32, (64, 64), 1)
    band = (chip + row // 16) & 3
    harmonic = BAND * band + (row & 7) + 1
    step = 64 * chip + ((lane + 32 * core) & 63)
    turns = (harmonic * step + 64 * ((row // 8) & 1)) & (TIME - 1)
    return jnp.cos(turns.astype(F32) * (2.0 * math.pi / TIME)) * (2.0 / TIME)


def params(mib=16):
    return pltpu.CompilerParams(vmem_limit_bytes=mib * MIB)


def split(value):
    high = value.astype(BF16)
    low = (value - high.astype(F32)).astype(BF16)
    return high, low


def source_kernel(series_ref, pack_ref, keep_ref, send_ref):
    core = lax.rem(lax.axis_index("obs"), 2)
    area = pack_ref[3:6, :] * (pack_ref[9:10, :] >= 0).astype(F32)
    for pair in range(HALF // 128):
        blocks = []
        for side in range(2):
            lanes = slice(128 * (2 * pair + side), 128 * (2 * pair + side) + 128)
            field = [series_ref[f, :, lanes] for f in range(5)]
            b1, b2, b3 = area[0:1, lanes], area[1:2, lanes], area[2:3, lanes]
            bc = MACH_NUMBER * b1
            flux = b1 * field[1] + b2 * field[2] + b3 * field[3] + bc * field[0]
            blocks.append([flux] + [b * field[4] + bc * field[1 + i] for i, b in enumerate((b1, b2, b3))])
        lanes = slice(128 * pair, 128 * pair + 128)
        for f in range(4):
            even, odd = blocks[0][f], blocks[1][f]
            rows = slice(32 * f, 32 * f + 32)
            keep_ref[rows, lanes] = jnp.where(core == 0, even, odd)
            send_ref[rows, lanes] = jnp.where(core == 0, odd, even)


def feature_kernel(pack_ref, out_ref):
    x = pack_ref[6:9, 0:OBSERVERS]
    rows = jnp.concatenate(
        [
            jnp.ones((1, OBSERVERS), F32),
            x,
            x[0:1] * x[0:1] + x[1:2] * x[1:2] + x[2:3] * x[2:3],
        ],
        axis=0,
    )
    high = rows.astype(BF16).astype(F32)
    low = rows - high
    rest = jnp.zeros((1, OBSERVERS), F32)
    out_ref[...] = jnp.concatenate([high, high, low, rest] * BAND, axis=0).astype(BF16)


def band_kernel(keep_ref, recv_ref, own_ref, up_ref, down_ref, far_ref, mark_ref):
    mark_ref[...] = jnp.zeros(mark_ref.shape, F32)
    high, low = split(fourier_rows())
    table = jnp.concatenate([high, high, low], axis=1)
    for f in range(4):
        rows = slice(32 * f, 32 * f + 32)
        for tile in range(HALF // 256):
            lanes = slice(256 * tile, 256 * tile + 256)
            kh, kl = split(keep_ref[rows, lanes])
            rh, rl = split(recv_ref[rows, lanes])
            stack = jnp.concatenate([kh, rh, kl, rl, kh, rh], axis=0)
            part = jnp.dot(table, stack, preferred_element_type=F32)
            out = slice(HALF * f + 256 * tile, HALF * f + 256 * tile + 256)
            own_ref[:, out] = part[0:16]
            up_ref[:, out] = part[16:32]
            down_ref[:, out] = part[48:64]
            far_ref[:, out] = part[32:48]


def double(cosine, sine):
    twice = cosine + cosine
    return twice * cosine - 1.0, twice * sine


def geometry_kernel(pack_ref, mark_ref, geo_ref, wide_ref):
    place = lax.axis_index("obs")
    core = lax.rem(place, 2)
    chip = lax.div(place, 2)

    def tile_step(power, first, t):
        lanes = pl.ds(pl.multiple_of(t * 128, 128), 128)
        x = [jnp.broadcast_to(pack_ref[6 + i : 7 + i, lanes], (8, 128)) for i in range(3)]
        for g in range(16):
            rows = pl.ds(pl.multiple_of(first + 8 * g, 8), 8)
            square = None
            for i in range(3):
                delta = x[i] - wide_ref[i, 8 * g : 8 * g + 8, :]
                square = delta * delta if square is None else square + delta * delta
            inverse = lax.rsqrt(square)
            r = square * inverse
            half = r * (0.5 * BASE) - 0.5 * math.pi
            s2 = half * half
            sine = s2 * SIN_FIT[-1] + SIN_FIT[-2]
            for c in SIN_FIT[-3::-1]:
                sine = sine * s2 + c
            sine = sine * half
            cosine = s2 * COS_FIT[-1] + COS_FIT[-2]
            for c in COS_FIT[-3::-1]:
                cosine = cosine * s2 + c
            twice = sine + sine
            er = twice * sine - 1.0
            ei = twice * cosine
            amp = inverse * inverse * (inverse * (1.0 / FOUR_PI))
            if power == 0:
                gr, gi = amp, jnp.zeros_like(amp)
            else:
                cr, ci = er, ei
                for _ in range(3):
                    cr, ci = double(cr, ci)
                if power == 2:
                    cr, ci = double(cr, ci)
                elif power == 3:
                    dr, di = double(cr, ci)
                    cr, ci = cr * dr - ci * di, cr * di + ci * dr
                gr, gi = amp * cr, amp * ci
            geo_ref[0, rows, lanes] = r
            geo_ref[1, rows, lanes] = er
            geo_ref[2, rows, lanes] = ei
            geo_ref[3, rows, lanes] = gr
            geo_ref[4, rows, lanes] = gi

    def body(power):
        def chunk(c, carry):
            wide = pl.multiple_of(c * 256, 256)
            pos = jnp.where(
                core == 0, pack_ref[0:3, pl.ds(wide, 128)], pack_ref[0:3, pl.ds(wide + 128, 128)]
            )
            pos = jnp.concatenate([pos, jnp.zeros((5, 128), F32)], axis=0)
            y = jnp.transpose(pos)
            for i in range(3):
                wide_ref[i] = jnp.broadcast_to(y[:, i : i + 1], (128, 128))

            def tile(t, inner):
                tile_step(power, c * 128, t)
                return inner

            lax.fori_loop(0, OBSERVERS // 128, tile, 0)
            return carry

        lax.fori_loop(0, HALF // 128, chunk, 0)

    for power in range(CHIPS):
        pl.when(chip == power)(lambda power=power: body(power))


def build_left(spec, pack_ref, stage, left):
    core = lax.rem(lax.axis_index("obs"), 2)
    first_band = lax.div(lax.axis_index("obs"), 2) * BAND
    wave = (lax.broadcasted_iota(jnp.int32, (BAND, 128), 0) + (first_band + 1)).astype(F32) * BASE
    freq_of = lax.broadcasted_iota(jnp.int32, (128, 128), 1) // 16
    stage[...] = jnp.zeros(stage.shape, F32)

    def chunk(c, carry):
        wide = pl.multiple_of(c * 256, 256)
        y = jnp.where(
            core == 0, pack_ref[0:3, pl.ds(wide, 128)], pack_ref[0:3, pl.ds(wide + 128, 128)]
        )
        y = [y[i : i + 1] for i in range(3)]
        square = y[0] * y[0] + y[1] * y[1] + y[2] * y[2]
        flux = spec(0, c)
        load = [spec(1 + i, c) for i in range(3)]
        gains = (-wave * flux[1], wave * flux[0])
        moment = [
            -(y[0] * load[0][p] + y[1] * load[1][p] + y[2] * load[2][p]) for p in range(2)
        ]
        comps = []
        for p in range(2):
            g = gains[p]
            rows = [g * square + moment[p]]
            rows += [load[i][p] - 2.0 * (y[i] * g) for i in range(3)]
            comps.append(rows + [g])
        for p in range(2):
            comps.append([wave * moment[p]] + [wave * load[i][p] for i in range(3)])
        for comp, rows in enumerate(comps):
            for q, row in enumerate(rows):
                high = row.astype(BF16).astype(F32)
                for place, value in ((q, high), (5 + q, row - high), (10 + q, high)):
                    stage[pl.ds(128 * comp + place, 8, stride=16), :] = value
        for comp in range(4):
            turned = jnp.transpose(stage[128 * comp : 128 * comp + 128, :])
            for k in range(BAND):
                block = jnp.where(freq_of == k, turned, 0.0).astype(BF16)
                left[pl.ds(c * 8, 8), comp * BAND + k] = block.reshape(8, GROUP, DEPTH)
        return carry

    lax.fori_loop(0, HALF // 128, chunk, 0)


def field_kernel(
    own_ref, up_ref, down_ref, far_ref, pack_ref, feature_ref,
    geo_ref,
    out_ref, stage, left, ready, after, total,
):
    def spec(f, c):
        lanes = pl.ds(pl.multiple_of(HALF * f + c * 128, 128), 128)
        value = own_ref[:, lanes] + up_ref[:, lanes] + (down_ref[:, lanes] + far_ref[:, lanes])
        return value[0:8], value[8:16]

    build_left(spec, pack_ref, stage, left)
    total[...] = jnp.zeros(total.shape, F32)
    batches = HALF // BATCH
    steps = batches * (OBSERVERS // LIST)
    groups = BATCH // GROUP

    def product(target, i, part):
        t, b = lax.div(i, batches), lax.rem(i, batches)
        size = 32 * GROUP * groups // PIECES
        if PIECES <= groups:
            lhs = left[pl.ds(b * groups + part * (groups // PIECES), groups // PIECES)]
        else:
            cut = PIECES // groups
            span = 32 // cut
            lhs = left[b * groups + part // cut, span * (part % cut) : span * (part % cut) + span]
        rhs = feature_ref[:, pl.ds(pl.multiple_of(t * LIST, LIST), LIST)]
        target[part * size : part * size + size] = jnp.dot(
            lhs.reshape(size, DEPTH), rhs, preferred_element_type=F32
        )

    def consume(source, i, target, following):
        t, b = lax.div(i, batches), lax.rem(i, batches)
        for lane in range(LIST // 128):
            lanes = pl.ds(pl.multiple_of(t * LIST + 128 * lane, 128), 128)
            near = slice(128 * lane, 128 * lane + 128)
            acc = [total[t, lane * 16 + i] for i in range(16)]
            for sub in range(BATCH // 8):
                piece, rest = divmod((lane * (BATCH // 8) + sub) * PIECES, BATCH // 4)
                if rest == 0:
                    product(target, following, piece)
                rows = pl.ds(pl.multiple_of(b * BATCH + 8 * sub, 8), 8)
                r, er, ei, pr, pi = [geo_ref[i, rows, lanes] for i in range(5)]
                cr, ci = pr * er - pi * ei, pr * ei + pi * er
                twice = er + er
                for k in range(BAND):
                    m = []
                    for comp in range(4):
                        base = ((sub // 2) * 32 + comp * BAND + k) * GROUP + 8 * (sub % 2)
                        m.append(source[base : base + 8, near])
                    tr = m[0] - r * m[3]
                    ti = m[1] + r * m[2]
                    acc[2 * k] = acc[2 * k] + (cr * tr - ci * ti)
                    acc[2 * k + 1] = acc[2 * k + 1] + (cr * ti + ci * tr)
                    if k + 1 < BAND:
                        pr, pi, cr, ci = cr, ci, twice * cr - pr, twice * ci - pi
            for i in range(16):
                total[t, lane * 16 + i] = acc[i]

    for part in range(PIECES):
        product(ready, 0, part)

    def step(i, carry):
        following = jnp.minimum(i + 1, steps - 1)

        @pl.when(lax.rem(i, 2) == 0)
        def _():
            consume(ready, i, after, following)

        @pl.when(lax.rem(i, 2) == 1)
        def _():
            consume(after, i, ready, following)

        return carry

    lax.fori_loop(0, steps, step, 0)

    lane_block = lax.broadcasted_iota(jnp.int32, (4, 128), 1) // 32
    for t in range(OBSERVERS // LIST):
        for lane in range(LIST // 128):
            sums = [jnp.sum(total[t, lane * 16 + i], axis=0, keepdims=True) for i in range(16)]
            packs = [
                jnp.concatenate(
                    [sums[2 * kk], sums[2 * kk + 1], sums[2 * (4 + kk)], sums[2 * (4 + kk) + 1]],
                    axis=0,
                )
                for kk in range(4)
            ]
            for m in range(4):
                value = None
                for kk in range(4):
                    shift = (32 * (kk - m)) % 128
                    turned = pltpu.roll(packs[kk], shift, axis=1) if shift else packs[kk]
                    value = turned if value is None else jnp.where(lane_block == kk, turned, value)
                for h in range(2):
                    out_ref[2 * (8 * t + 4 * lane + m) + h] = value[2 * h : 2 * h + 2]


def finish_kernel(parts_ref, out_ref):
    value = jnp.sum(parts_ref[...], axis=0)
    for kk in range(4):
        out_ref[:, kk, :] = value[:, 32 * kk : 32 * kk + 32]


def shape(*dims, dtype=F32):
    return jax.ShapeDtypeStruct(dims, dtype)


def on_device(series, panel_pos, panel_area, observers, owner):
    whole = pl.BlockSpec(memory_space=pltpu.VMEM)
    pack = jnp.concatenate(
        [
            panel_pos,
            panel_area,
            jnp.pad(observers, ((0, 0), (0, SLOTS - OBSERVERS))),
            owner.astype(F32).reshape(1, SLOTS),
        ],
        axis=0,
    )
    keep, send = pl.pallas_call(
        source_kernel,
        out_shape=(shape(128, HALF), shape(128, HALF)),
        in_specs=[whole] * 2,
        out_specs=(whole,) * 2,
        compiler_params=params(),
        name="sources",
    )(jnp.transpose(series, (1, 0, 2)), pack)
    features = pl.pallas_call(
        feature_kernel,
        out_shape=shape(DEPTH, OBSERVERS, dtype=BF16),
        in_specs=[whole],
        out_specs=whole,
        compiler_params=params(),
        name="features",
    )(pack)
    swap = [(i, i ^ 1) for i in range(8)]
    above = [(i, (i + 2) % 8) for i in range(8)]
    below = [(i, (i + 6) % 8) for i in range(8)]
    recv = lax.ppermute(send, "obs", swap)

    pair_count = HALF * OBSERVERS
    own, up, down, far, mark = pl.pallas_call(
        band_kernel,
        out_shape=(shape(16, 4 * HALF),) * 4 + (shape(8, 128),),
        in_specs=[whole] * 2,
        out_specs=(whole,) * 5,
        compiler_params=params(),
        name="bands",
    )(keep, recv)

    geometry = pl.pallas_call(
        geometry_kernel,
        out_shape=shape(5, HALF, OBSERVERS),
        in_specs=[whole] * 2,
        out_specs=whole,
        scratch_shapes=[pltpu.VMEM((3, 128, 128), F32)],
        compiler_params=params(8),
        cost_estimate=pl.CostEstimate(
            flops=80 * pair_count, bytes_accessed=32 * MIB, transcendentals=0
        ),
        name="geometry",
    )(pack, mark)
    across = lax.ppermute(far, "obs", [(i, (i + 4) % 8) for i in range(8)])
    from_below = lax.ppermute(up, "obs", above)
    from_above = lax.ppermute(down, "obs", below)

    chunks = pl.pallas_call(
        field_kernel,
        out_shape=shape(64, 2, 128),
        in_specs=[whole] * 7,
        out_specs=whole,
        scratch_shapes=[
            pltpu.VMEM((512, 128), F32),
            pltpu.VMEM((HALF // GROUP, 32, GROUP, DEPTH), BF16),
            pltpu.VMEM((32 * BATCH, LIST), F32),
            pltpu.VMEM((32 * BATCH, LIST), F32),
            pltpu.VMEM((OBSERVERS // LIST, 32, 8, 128), F32),
        ],
        compiler_params=params(32),
        name="field",
    )(own, from_below, from_above, across, pack, features, geometry)

    members = [
        [8 * d + 2 * y + c for d in range(lax.axis_size("panel")) for c in range(2)]
        for y in range(CHIPS)
    ]
    parts = lax.all_to_all(
        chunks,
        ("panel", "obs"),
        split_axis=0,
        concat_axis=0,
        axis_index_groups=members,
        tiled=True,
    )
    value = pl.pallas_call(
        finish_kernel,
        out_shape=shape(2, 4, 32),
        in_specs=[whole],
        out_specs=whole,
        compiler_params=params(),
        name="finish",
    )(parts)
    return jnp.transpose(value, (2, 0, 1))


def solution(mesh):
    in_specs = (P("obs", None, "panel"), P(None, "panel"), P(None, "panel"), P(), P("panel"))
    out_specs = P("panel", None, "obs")
    return jax.shard_map(
        on_device, mesh=mesh, in_specs=in_specs, out_specs=out_specs, check_vma=False
    )
```

```python
import functools
import math

import jax
import jax.numpy as jnp
import numpy as np
from jax import lax
from jax.experimental import pallas as pl
from jax.experimental.pallas import tpu as pltpu
from jax.sharding import PartitionSpec as P

TIME = 256
FREQ = 32
MACH_NUMBER = 0.3
SAMPLE_SPACING = 0.04
FOUR_PI = 4.0 * math.pi
BASE = 2.0 * math.pi / (TIME * SAMPLE_SPACING)

OBSERVERS = 1024
SLOTS = 2048
HALF = SLOTS // 2
STEPS = 32
CHIPS = 4
BAND = 8
LIST = 256
GROUP = 16
BATCH = 256
PIECES = 16
EARLY = 1
DEPTH = 128
MIB = 1 << 20

F32 = jnp.float32
BF16 = jnp.bfloat16


def sine_fits():
    node = np.cos((np.arange(400) + 0.5) * np.pi / 400) * 0.5 + 0.5
    square = node * 0.66**2
    angle = np.sqrt(square)
    table = []
    for values, degree in ((np.sin(angle) / angle, 3), (np.cos(angle), 4)):
        fit = np.polynomial.chebyshev.Chebyshev.fit(square, values, degree, domain=[0, 0.66**2])
        table.append([float(v) for v in fit.convert(kind=np.polynomial.Polynomial).coef])
    return table


SIN_FIT, COS_FIT = sine_fits()


def fourier_rows():
    place = lax.axis_index("obs")
    chip, core = lax.div(place, 2), lax.rem(place, 2)
    row = lax.broadcasted_iota(jnp.int32, (64, 64), 0)
    lane = lax.broadcasted_iota(jnp.int32, (64, 64), 1)
    band = (chip + row // 16) & 3
    harmonic = BAND * band + (row & 7) + 1
    step = 64 * chip + ((lane + 32 * core) & 63)
    turns = (harmonic * step + 64 * ((row // 8) & 1)) & (TIME - 1)
    return jnp.cos(turns.astype(F32) * (2.0 * math.pi / TIME)) * (2.0 / TIME)


def params(mib=16):
    return pltpu.CompilerParams(vmem_limit_bytes=mib * MIB)


def split(value):
    high = value.astype(BF16)
    low = (value - high.astype(F32)).astype(BF16)
    return high, low


def source_kernel(series_ref, pack_ref, keep_ref, send_ref, mark_ref):
    mark_ref[...] = jnp.zeros(mark_ref.shape, F32)
    core = lax.rem(lax.axis_index("obs"), 2)
    area = pack_ref[3:6, :] * (pack_ref[9:10, :] >= 0).astype(F32)
    for pair in range(HALF // 128):
        blocks = []
        for side in range(2):
            lanes = slice(128 * (2 * pair + side), 128 * (2 * pair + side) + 128)
            field = [series_ref[f, :, lanes] for f in range(5)]
            b1, b2, b3 = area[0:1, lanes], area[1:2, lanes], area[2:3, lanes]
            bc = MACH_NUMBER * b1
            flux = b1 * field[1] + b2 * field[2] + b3 * field[3] + bc * field[0]
            blocks.append([flux] + [b * field[4] + bc * field[1 + i] for i, b in enumerate((b1, b2, b3))])
        lanes = slice(128 * pair, 128 * pair + 128)
        for f in range(4):
            even, odd = blocks[0][f], blocks[1][f]
            rows = slice(32 * f, 32 * f + 32)
            keep_ref[rows, lanes] = jnp.where(core == 0, even, odd)
            send_ref[rows, lanes] = jnp.where(core == 0, odd, even)


def feature_kernel(pack_ref, out_ref):
    x = pack_ref[6:9, 0:OBSERVERS]
    rows = jnp.concatenate(
        [
            jnp.ones((1, OBSERVERS), F32),
            x,
            x[0:1] * x[0:1] + x[1:2] * x[1:2] + x[2:3] * x[2:3],
        ],
        axis=0,
    )
    high = rows.astype(BF16).astype(F32)
    low = rows - high
    rest = jnp.zeros((1, OBSERVERS), F32)
    out_ref[...] = jnp.concatenate([high, high, low, rest] * BAND, axis=0).astype(BF16)


def band_kernel(keep_ref, recv_ref, given_ref, own_ref, up_ref, down_ref, far_ref, mark_ref):
    mark_ref[...] = given_ref[...]
    high, low = split(fourier_rows())
    table = jnp.concatenate([high, high, low], axis=1)
    for f in range(4):
        rows = slice(32 * f, 32 * f + 32)
        for tile in range(HALF // 256):
            lanes = slice(256 * tile, 256 * tile + 256)
            kh, kl = split(keep_ref[rows, lanes])
            rh, rl = split(recv_ref[rows, lanes])
            stack = jnp.concatenate([kh, rh, kl, rl, kh, rh], axis=0)
            part = jnp.dot(table, stack, preferred_element_type=F32)
            out = slice(HALF * f + 256 * tile, HALF * f + 256 * tile + 256)
            own_ref[:, out] = part[0:16]
            up_ref[:, out] = part[16:32]
            down_ref[:, out] = part[48:64]
            far_ref[:, out] = part[32:48]


def double(cosine, sine):
    twice = cosine + cosine
    return twice * cosine - 1.0, twice * sine


def early_kernel(pack_ref, mark_ref, geo_ref, done_ref, wide_ref):
    done_ref[...] = mark_ref[...]
    geometry_chunks(0, EARLY, pack_ref, geo_ref, wide_ref)


def geometry_kernel(pack_ref, mark_ref, early_ref, geo_ref, wide_ref):
    for i in range(6):
        geo_ref[i, 0 : 128 * EARLY, :] = early_ref[i]
    geometry_chunks(EARLY, HALF // 128, pack_ref, geo_ref, wide_ref)


def geometry_chunks(first_chunk, last_chunk, pack_ref, geo_ref, wide_ref):
    place = lax.axis_index("obs")
    core = lax.rem(place, 2)
    chip = lax.div(place, 2)

    def tile_step(power, first, t):
        lanes = pl.ds(pl.multiple_of(t * 128, 128), 128)
        x = [jnp.broadcast_to(pack_ref[6 + i : 7 + i, lanes], (8, 128)) for i in range(3)]
        for g in range(16):
            rows = pl.ds(pl.multiple_of(first + 8 * g, 8), 8)
            square = None
            for i in range(3):
                delta = x[i] - wide_ref[i, 8 * g : 8 * g + 8, :]
                square = delta * delta if square is None else square + delta * delta
            inverse = lax.rsqrt(square)
            r = square * inverse
            quarter = r * (0.25 * BASE) - 0.25 * math.pi
            s2 = quarter * quarter
            sine = s2 * SIN_FIT[-1] + SIN_FIT[-2]
            for c in SIN_FIT[-3::-1]:
                sine = sine * s2 + c
            sine = sine * quarter
            cosine = s2 * COS_FIT[-1] + COS_FIT[-2]
            for c in COS_FIT[-3::-1]:
                cosine = cosine * s2 + c
            cosine, sine = double(cosine, sine)
            twice = sine + sine
            er = twice * sine - 1.0
            ei = twice * cosine
            amp = inverse * inverse * (inverse * (1.0 / FOUR_PI))
            if power == 0:
                gr, gi = amp, jnp.zeros_like(amp)
            else:
                cr, ci = er, ei
                for _ in range(3):
                    cr, ci = double(cr, ci)
                if power == 2:
                    cr, ci = double(cr, ci)
                elif power == 3:
                    dr, di = double(cr, ci)
                    cr, ci = cr * dr - ci * di, cr * di + ci * dr
                gr, gi = amp * cr, amp * ci
            br, bi = (gr * er, gr * ei) if power == 0 else (gr * er - gi * ei, gr * ei + gi * er)
            for i, value in enumerate((r, er + er, gr, gi, br, bi)):
                geo_ref[i, rows, lanes] = value

    def body(power):
        def chunk(c, carry):
            wide = pl.multiple_of(c * 256, 256)
            pos = jnp.where(
                core == 0, pack_ref[0:3, pl.ds(wide, 128)], pack_ref[0:3, pl.ds(wide + 128, 128)]
            )
            pos = jnp.concatenate([pos, jnp.zeros((5, 128), F32)], axis=0)
            y = jnp.transpose(pos)
            for i in range(3):
                wide_ref[i] = jnp.broadcast_to(y[:, i : i + 1], (128, 128))

            def tile(t, inner):
                tile_step(power, c * 128, t)
                return inner

            lax.fori_loop(0, OBSERVERS // 128, tile, 0)
            return carry

        lax.fori_loop(first_chunk, last_chunk, chunk, 0)

    for power in range(CHIPS):
        pl.when(chip == power)(lambda power=power: body(power))


def build_left(spec, pack_ref, stage, left):
    core = lax.rem(lax.axis_index("obs"), 2)
    first_band = lax.div(lax.axis_index("obs"), 2) * BAND
    wave = (lax.broadcasted_iota(jnp.int32, (BAND, 128), 0) + (first_band + 1)).astype(F32) * BASE
    freq_of = lax.broadcasted_iota(jnp.int32, (128, 128), 1) // 16
    stage[...] = jnp.zeros(stage.shape, F32)

    def chunk(c, carry):
        wide = pl.multiple_of(c * 256, 256)
        y = jnp.where(
            core == 0, pack_ref[0:3, pl.ds(wide, 128)], pack_ref[0:3, pl.ds(wide + 128, 128)]
        )
        y = [y[i : i + 1] for i in range(3)]
        square = y[0] * y[0] + y[1] * y[1] + y[2] * y[2]
        flux = spec(0, c)
        load = [spec(1 + i, c) for i in range(3)]
        gains = (-wave * flux[1], wave * flux[0])
        moment = [
            -(y[0] * load[0][p] + y[1] * load[1][p] + y[2] * load[2][p]) for p in range(2)
        ]
        comps = []
        for p in range(2):
            g = gains[p]
            rows = [g * square + moment[p]]
            rows += [load[i][p] - 2.0 * (y[i] * g) for i in range(3)]
            comps.append(rows + [g])
        for p in range(2):
            comps.append([wave * moment[p]] + [wave * load[i][p] for i in range(3)])
        for comp, rows in enumerate(comps):
            for q, row in enumerate(rows):
                high = row.astype(BF16).astype(F32)
                for place, value in ((q, high), (5 + q, row - high), (10 + q, high)):
                    stage[pl.ds(128 * comp + place, 8, stride=16), :] = value
        for comp in range(4):
            turned = jnp.transpose(stage[128 * comp : 128 * comp + 128, :])
            for k in range(BAND):
                block = jnp.where(freq_of == k, turned, 0.0).astype(BF16)
                left[pl.ds(c * 8, 8), comp * BAND + k] = block.reshape(8, GROUP, DEPTH)
        return carry

    lax.fori_loop(0, HALF // 128, chunk, 0)


def field_kernel(
    own_ref, up_ref, down_ref, far_ref, pack_ref, feature_ref,
    geo_ref,
    out_ref, stage, left, ready, after, total,
):
    def spec(f, c):
        lanes = pl.ds(pl.multiple_of(HALF * f + c * 128, 128), 128)
        value = own_ref[:, lanes] + up_ref[:, lanes] + (down_ref[:, lanes] + far_ref[:, lanes])
        return value[0:8], value[8:16]

    build_left(spec, pack_ref, stage, left)
    total[...] = jnp.zeros(total.shape, F32)
    batches = HALF // BATCH
    steps = batches * (OBSERVERS // LIST)
    groups = BATCH // GROUP

    def product(target, i, part):
        t, b = lax.div(i, batches), lax.rem(i, batches)
        size = 32 * GROUP * groups // PIECES
        if PIECES <= groups:
            lhs = left[pl.ds(b * groups + part * (groups // PIECES), groups // PIECES)]
        else:
            cut = PIECES // groups
            span = 32 // cut
            lhs = left[b * groups + part // cut, span * (part % cut) : span * (part % cut) + span]
        rhs = feature_ref[:, pl.ds(pl.multiple_of(t * LIST, LIST), LIST)]
        target[part * size : part * size + size] = jnp.dot(
            lhs.reshape(size, DEPTH), rhs, preferred_element_type=F32
        )

    def consume(source, i, target, following):
        t, b = lax.div(i, batches), lax.rem(i, batches)
        sums = []
        for lane in range(LIST // 128):
            lanes = pl.ds(pl.multiple_of(t * LIST + 128 * lane, 128), 128)
            near = slice(128 * lane, 128 * lane + 128)
            acc = [None] * 16
            for sub in range(BATCH // 8):
                piece, rest = divmod((lane * (BATCH // 8) + sub) * PIECES, BATCH // 4)
                if rest == 0:
                    product(target, following, piece)
                rows = pl.ds(pl.multiple_of(b * BATCH + 8 * sub, 8), 8)
                r, twice, pr, pi, cr, ci = [geo_ref[i, rows, lanes] for i in range(6)]
                for k in range(BAND):
                    m = []
                    for comp in range(4):
                        base = ((sub // 2) * 32 + comp * BAND + k) * GROUP + 8 * (sub % 2)
                        m.append(source[base : base + 8, near])
                    tr = m[0] - r * m[3]
                    ti = m[1] + r * m[2]
                    for slot, term in ((2 * k, cr * tr - ci * ti), (2 * k + 1, cr * ti + ci * tr)):
                        acc[slot] = term if acc[slot] is None else acc[slot] + term
                    if k + 1 < BAND:
                        pr, pi, cr, ci = cr, ci, twice * cr - pr, twice * ci - pi
            sums += acc
        for i in range(32):
            total[t, i] = total[t, i] + sums[i]

    for part in range(PIECES):
        product(ready, 0, part)

    def step(i, carry):
        following = jnp.minimum(i + 1, steps - 1)

        @pl.when(lax.rem(i, 2) == 0)
        def _():
            consume(ready, i, after, following)

        @pl.when(lax.rem(i, 2) == 1)
        def _():
            consume(after, i, ready, following)

        return carry

    lax.fori_loop(0, steps, step, 0)

    lane_block = lax.broadcasted_iota(jnp.int32, (4, 128), 1) // 32
    for t in range(OBSERVERS // LIST):
        for lane in range(LIST // 128):
            sums = [jnp.sum(total[t, lane * 16 + i], axis=0, keepdims=True) for i in range(16)]
            packs = [
                jnp.concatenate(
                    [sums[2 * kk], sums[2 * kk + 1], sums[2 * (4 + kk)], sums[2 * (4 + kk) + 1]],
                    axis=0,
                )
                for kk in range(4)
            ]
            for m in range(4):
                value = None
                for kk in range(4):
                    shift = (32 * (kk - m)) % 128
                    turned = pltpu.roll(packs[kk], shift, axis=1) if shift else packs[kk]
                    value = turned if value is None else jnp.where(lane_block == kk, turned, value)
                for h in range(2):
                    out_ref[2 * (8 * t + 4 * lane + m) + h] = value[2 * h : 2 * h + 2]


def finish_kernel(parts_ref, out_ref):
    value = jnp.sum(parts_ref[...], axis=0)
    for kk in range(4):
        out_ref[:, kk, :] = value[:, 32 * kk : 32 * kk + 32]


def shape(*dims, dtype=F32):
    return jax.ShapeDtypeStruct(dims, dtype)


def on_device(series, panel_pos, panel_area, observers, owner):
    whole = pl.BlockSpec(memory_space=pltpu.VMEM)
    pack = jnp.concatenate(
        [
            panel_pos,
            panel_area,
            jnp.pad(observers, ((0, 0), (0, SLOTS - OBSERVERS))),
            owner.astype(F32).reshape(1, SLOTS),
        ],
        axis=0,
    )
    keep, send, begun = pl.pallas_call(
        source_kernel,
        out_shape=(shape(128, HALF), shape(128, HALF), shape(8, 128)),
        in_specs=[whole] * 2,
        out_specs=(whole,) * 3,
        compiler_params=params(),
        name="sources",
    )(jnp.transpose(series, (1, 0, 2)), pack)
    features = pl.pallas_call(
        feature_kernel,
        out_shape=shape(DEPTH, OBSERVERS, dtype=BF16),
        in_specs=[whole],
        out_specs=whole,
        compiler_params=params(),
        name="features",
    )(pack)
    swap = [(i, i ^ 1) for i in range(8)]
    above = [(i, (i + 2) % 8) for i in range(8)]
    below = [(i, (i + 6) % 8) for i in range(8)]
    recv = lax.ppermute(send, "obs", swap)

    pair_count = HALF * OBSERVERS
    early, ready = pl.pallas_call(
        early_kernel,
        out_shape=(shape(6, 128 * EARLY, OBSERVERS), shape(8, 128)),
        in_specs=[whole] * 2,
        out_specs=(whole, whole),
        scratch_shapes=[pltpu.VMEM((3, 128, 128), F32)],
        compiler_params=params(8),
        cost_estimate=pl.CostEstimate(
            flops=10 * pair_count, bytes_accessed=4 * MIB, transcendentals=0
        ),
        name="early",
    )(pack, begun)
    own, up, down, far, mark = pl.pallas_call(
        band_kernel,
        out_shape=(shape(16, 4 * HALF),) * 4 + (shape(8, 128),),
        in_specs=[whole] * 3,
        out_specs=(whole,) * 5,
        compiler_params=params(),
        name="bands",
    )(keep, recv, ready)

    geometry = pl.pallas_call(
        geometry_kernel,
        out_shape=shape(6, HALF, OBSERVERS),
        in_specs=[whole] * 3,
        out_specs=whole,
        scratch_shapes=[pltpu.VMEM((3, 128, 128), F32)],
        compiler_params=params(8),
        cost_estimate=pl.CostEstimate(
            flops=80 * pair_count, bytes_accessed=32 * MIB, transcendentals=0
        ),
        name="geometry",
    )(pack, mark, early)
    across = lax.ppermute(far, "obs", [(i, (i + 4) % 8) for i in range(8)])
    from_below = lax.ppermute(up, "obs", above)
    from_above = lax.ppermute(down, "obs", below)

    chunks = pl.pallas_call(
        field_kernel,
        out_shape=shape(64, 2, 128),
        in_specs=[whole] * 7,
        out_specs=whole,
        scratch_shapes=[
            pltpu.VMEM((512, 128), F32),
            pltpu.VMEM((HALF // GROUP, 32, GROUP, DEPTH), BF16),
            pltpu.VMEM((32 * BATCH, LIST), F32),
            pltpu.VMEM((32 * BATCH, LIST), F32),
            pltpu.VMEM((OBSERVERS // LIST, 32, 8, 128), F32),
        ],
        compiler_params=params(28),
        name="field",
    )(own, from_below, from_above, across, pack, features, geometry)

    members = [
        [8 * d + 2 * y + c for d in range(lax.axis_size("panel")) for c in range(2)]
        for y in range(CHIPS)
    ]
    parts = lax.all_to_all(
        chunks,
        ("panel", "obs"),
        split_axis=0,
        concat_axis=0,
        axis_index_groups=members,
        tiled=True,
    )
    value = pl.pallas_call(
        finish_kernel,
        out_shape=shape(2, 4, 32),
        in_specs=[whole],
        out_specs=whole,
        compiler_params=params(),
        name="finish",
    )(parts)
    return jnp.transpose(value, (2, 0, 1))


def solution(mesh):
    in_specs = (P("obs", None, "panel"), P(None, "panel"), P(None, "panel"), P(), P("panel"))
    out_specs = P("panel", None, "obs")
    return jax.shard_map(
        on_device, mesh=mesh, in_specs=in_specs, out_specs=out_specs, check_vma=False
    )
```

```python
import functools
import math

import jax
import jax.numpy as jnp
import numpy as np
from jax import lax
from jax.experimental import pallas as pl
from jax.experimental.pallas import tpu as pltpu
from jax.sharding import PartitionSpec as P

TIME = 256
FREQ = 32
MACH_NUMBER = 0.3
SAMPLE_SPACING = 0.04
FOUR_PI = 4.0 * math.pi
BASE = 2.0 * math.pi / (TIME * SAMPLE_SPACING)

OBSERVERS = 1024
SLOTS = 2048
HALF = SLOTS // 2
STEPS = 32
CHIPS = 4
BAND = 8
LIST = 256
GROUP = 16
BATCH = 256
PIECES = 16
EARLY = 1
DEPTH = 128
MIB = 1 << 20

F32 = jnp.float32
BF16 = jnp.bfloat16


def sine_fits():
    node = np.cos((np.arange(400) + 0.5) * np.pi / 400) * 0.5 + 0.5
    square = node * 0.66**2
    angle = np.sqrt(square)
    table = []
    for values, degree in ((np.sin(angle) / angle, 3), (np.cos(angle), 4)):
        fit = np.polynomial.chebyshev.Chebyshev.fit(square, values, degree, domain=[0, 0.66**2])
        table.append([float(v) for v in fit.convert(kind=np.polynomial.Polynomial).coef])
    return table


SIN_FIT, COS_FIT = sine_fits()


def fourier_rows():
    place = lax.axis_index("obs")
    chip, core = lax.div(place, 2), lax.rem(place, 2)
    row = lax.broadcasted_iota(jnp.int32, (64, 64), 0)
    lane = lax.broadcasted_iota(jnp.int32, (64, 64), 1)
    band = (chip + row // 16) & 3
    harmonic = BAND * band + (row & 7) + 1
    step = 64 * chip + ((lane + 32 * core) & 63)
    turns = (harmonic * step + 64 * ((row // 8) & 1)) & (TIME - 1)
    return jnp.cos(turns.astype(F32) * (2.0 * math.pi / TIME)) * (2.0 / TIME)


def params(mib=16):
    return pltpu.CompilerParams(vmem_limit_bytes=mib * MIB)


def split(value):
    high = value.astype(BF16)
    low = (value - high.astype(F32)).astype(BF16)
    return high, low


def source_kernel(series_ref, pack_ref, keep_ref, send_ref, mark_ref):
    mark_ref[...] = jnp.zeros(mark_ref.shape, F32)
    core = lax.rem(lax.axis_index("obs"), 2)
    area = pack_ref[3:6, :] * (pack_ref[9:10, :] >= 0).astype(F32)
    for pair in range(HALF // 128):
        blocks = []
        for side in range(2):
            lanes = slice(128 * (2 * pair + side), 128 * (2 * pair + side) + 128)
            field = [series_ref[f, :, lanes] for f in range(5)]
            b1, b2, b3 = area[0:1, lanes], area[1:2, lanes], area[2:3, lanes]
            bc = MACH_NUMBER * b1
            flux = b1 * field[1] + b2 * field[2] + b3 * field[3] + bc * field[0]
            blocks.append([flux] + [b * field[4] + bc * field[1 + i] for i, b in enumerate((b1, b2, b3))])
        lanes = slice(128 * pair, 128 * pair + 128)
        for f in range(4):
            even, odd = blocks[0][f], blocks[1][f]
            rows = slice(32 * f, 32 * f + 32)
            keep_ref[rows, lanes] = jnp.where(core == 0, even, odd)
            send_ref[rows, lanes] = jnp.where(core == 0, odd, even)


def feature_kernel(pack_ref, out_ref):
    x = pack_ref[6:9, 0:OBSERVERS]
    rows = jnp.concatenate(
        [
            jnp.ones((1, OBSERVERS), F32),
            x,
            x[0:1] * x[0:1] + x[1:2] * x[1:2] + x[2:3] * x[2:3],
        ],
        axis=0,
    )
    high = rows.astype(BF16).astype(F32)
    low = rows - high
    rest = jnp.zeros((1, OBSERVERS), F32)
    out_ref[...] = jnp.concatenate([high, high, low, rest] * BAND, axis=0).astype(BF16)


def band_kernel(keep_ref, recv_ref, given_ref, own_ref, up_ref, down_ref, far_ref, mark_ref):
    mark_ref[...] = given_ref[...]
    high, low = split(fourier_rows())
    table = jnp.concatenate([high, high, low], axis=1)
    for f in range(4):
        rows = slice(32 * f, 32 * f + 32)
        for tile in range(HALF // 256):
            lanes = slice(256 * tile, 256 * tile + 256)
            kh, kl = split(keep_ref[rows, lanes])
            rh, rl = split(recv_ref[rows, lanes])
            stack = jnp.concatenate([kh, rh, kl, rl, kh, rh], axis=0)
            part = jnp.dot(table, stack, preferred_element_type=F32)
            out = slice(HALF * f + 256 * tile, HALF * f + 256 * tile + 256)
            own_ref[:, out] = part[0:16]
            up_ref[:, out] = part[16:32]
            down_ref[:, out] = part[48:64]
            far_ref[:, out] = part[32:48]


def double(cosine, sine):
    twice = cosine + cosine
    return twice * cosine - 1.0, twice * sine


def early_kernel(pack_ref, mark_ref, geo_ref, done_ref, wide_ref):
    done_ref[...] = mark_ref[...]
    geometry_chunks(0, EARLY, pack_ref, geo_ref, wide_ref)


def geometry_kernel(pack_ref, mark_ref, early_ref, geo_ref, wide_ref):
    for i in range(6):
        geo_ref[i, 0 : 128 * EARLY, :] = early_ref[i]
    geometry_chunks(EARLY, HALF // 128, pack_ref, geo_ref, wide_ref)


def geometry_chunks(first_chunk, last_chunk, pack_ref, geo_ref, wide_ref):
    place = lax.axis_index("obs")
    core = lax.rem(place, 2)
    chip = lax.div(place, 2)

    def tile_step(power, first, t):
        lanes = pl.ds(pl.multiple_of(t * 128, 128), 128)
        x = [jnp.broadcast_to(pack_ref[6 + i : 7 + i, lanes], (8, 128)) for i in range(3)]
        for g in range(16):
            rows = pl.ds(pl.multiple_of(first + 8 * g, 8), 8)
            square = None
            for i in range(3):
                delta = x[i] - wide_ref[i, 8 * g : 8 * g + 8, :]
                square = delta * delta if square is None else square + delta * delta
            inverse = lax.rsqrt(square)
            r = square * inverse
            quarter = r * (0.25 * BASE) - 0.25 * math.pi
            s2 = quarter * quarter
            sine = s2 * SIN_FIT[-1] + SIN_FIT[-2]
            for c in SIN_FIT[-3::-1]:
                sine = sine * s2 + c
            sine = sine * quarter
            cosine = s2 * COS_FIT[-1] + COS_FIT[-2]
            for c in COS_FIT[-3::-1]:
                cosine = cosine * s2 + c
            cosine, sine = double(cosine, sine)
            twice = sine + sine
            er = twice * sine - 1.0
            ei = twice * cosine
            amp = inverse * inverse * (inverse * (1.0 / FOUR_PI))
            if power == 0:
                gr, gi = amp, jnp.zeros_like(amp)
            else:
                cr, ci = er, ei
                for _ in range(3):
                    cr, ci = double(cr, ci)
                if power == 2:
                    cr, ci = double(cr, ci)
                elif power == 3:
                    dr, di = double(cr, ci)
                    cr, ci = cr * dr - ci * di, cr * di + ci * dr
                gr, gi = amp * cr, amp * ci
            br, bi = (gr * er, gr * ei) if power == 0 else (gr * er - gi * ei, gr * ei + gi * er)
            for i, value in enumerate((r, er + er, gr, gi, br, bi)):
                geo_ref[i, rows, lanes] = value

    def body(power):
        def chunk(c, carry):
            wide = pl.multiple_of(c * 256, 256)
            pos = jnp.where(
                core == 0, pack_ref[0:3, pl.ds(wide, 128)], pack_ref[0:3, pl.ds(wide + 128, 128)]
            )
            pos = jnp.concatenate([pos, jnp.zeros((5, 128), F32)], axis=0)
            y = jnp.transpose(pos)
            for i in range(3):
                wide_ref[i] = jnp.broadcast_to(y[:, i : i + 1], (128, 128))

            def tile(t, inner):
                tile_step(power, c * 128, t)
                return inner

            lax.fori_loop(0, OBSERVERS // 128, tile, 0)
            return carry

        lax.fori_loop(first_chunk, last_chunk, chunk, 0)

    for power in range(CHIPS):
        pl.when(chip == power)(lambda power=power: body(power))


def build_left(spec, pack_ref, stage, left):
    core = lax.rem(lax.axis_index("obs"), 2)
    first_band = lax.div(lax.axis_index("obs"), 2) * BAND
    wave = (lax.broadcasted_iota(jnp.int32, (BAND, 128), 0) + (first_band + 1)).astype(F32) * BASE
    freq_of = lax.broadcasted_iota(jnp.int32, (128, 128), 1) // 16
    stage[...] = jnp.zeros(stage.shape, F32)

    def chunk(c, carry):
        wide = pl.multiple_of(c * 256, 256)
        y = jnp.where(
            core == 0, pack_ref[0:3, pl.ds(wide, 128)], pack_ref[0:3, pl.ds(wide + 128, 128)]
        )
        y = [y[i : i + 1] for i in range(3)]
        square = y[0] * y[0] + y[1] * y[1] + y[2] * y[2]
        flux = spec(0, c)
        load = [spec(1 + i, c) for i in range(3)]
        gains = (-wave * flux[1], wave * flux[0])
        moment = [
            -(y[0] * load[0][p] + y[1] * load[1][p] + y[2] * load[2][p]) for p in range(2)
        ]
        comps = []
        for p in range(2):
            g = gains[p]
            rows = [g * square + moment[p]]
            rows += [load[i][p] - 2.0 * (y[i] * g) for i in range(3)]
            comps.append(rows + [g])
        for p in range(2):
            comps.append([wave * moment[p]] + [wave * load[i][p] for i in range(3)])
        for comp, rows in enumerate(comps):
            for q, row in enumerate(rows):
                high = row.astype(BF16).astype(F32)
                for place, value in ((q, high), (5 + q, row - high), (10 + q, high)):
                    stage[pl.ds(128 * comp + place, 8, stride=16), :] = value
        for comp in range(4):
            turned = jnp.transpose(stage[128 * comp : 128 * comp + 128, :])
            for k in range(BAND):
                block = jnp.where(freq_of == k, turned, 0.0).astype(BF16)
                left[pl.ds(c * 8, 8), comp * BAND + k] = block.reshape(8, GROUP, DEPTH)
        return carry

    return chunk


def field_kernel(
    own_ref, up_ref, down_ref, far_ref, pack_ref, feature_ref,
    geo_ref,
    out_ref, stage, left, ready, after, total,
):
    def spec(f, c):
        lanes = pl.ds(pl.multiple_of(HALF * f + c * 128, 128), 128)
        value = own_ref[:, lanes] + up_ref[:, lanes] + (down_ref[:, lanes] + far_ref[:, lanes])
        return value[0:8], value[8:16]

    chunk = build_left(spec, pack_ref, stage, left)
    total[...] = jnp.zeros(total.shape, F32)
    batches = HALF // BATCH
    steps = batches * (OBSERVERS // LIST)
    groups = BATCH // GROUP

    def product(target, i, part):
        t, b = lax.div(i, batches), lax.rem(i, batches)
        size = 32 * GROUP * groups // PIECES
        if PIECES <= groups:
            lhs = left[pl.ds(b * groups + part * (groups // PIECES), groups // PIECES)]
        else:
            cut = PIECES // groups
            span = 32 // cut
            lhs = left[b * groups + part // cut, span * (part % cut) : span * (part % cut) + span]
        rhs = feature_ref[:, pl.ds(pl.multiple_of(t * LIST, LIST), LIST)]
        target[part * size : part * size + size] = jnp.dot(
            lhs.reshape(size, DEPTH), rhs, preferred_element_type=F32
        )

    def consume(source, i, target, following):
        t, b = lax.div(i, batches), lax.rem(i, batches)
        sums = []
        for lane in range(LIST // 128):
            lanes = pl.ds(pl.multiple_of(t * LIST + 128 * lane, 128), 128)
            near = slice(128 * lane, 128 * lane + 128)
            acc = [None] * 16
            for sub in range(BATCH // 8):
                piece, rest = divmod((lane * (BATCH // 8) + sub) * PIECES, BATCH // 4)
                if rest == 0:
                    product(target, following, piece)
                rows = pl.ds(pl.multiple_of(b * BATCH + 8 * sub, 8), 8)
                r, twice, pr, pi, cr, ci = [geo_ref[i, rows, lanes] for i in range(6)]
                for k in range(BAND):
                    m = []
                    for comp in range(4):
                        base = ((sub // 2) * 32 + comp * BAND + k) * GROUP + 8 * (sub % 2)
                        m.append(source[base : base + 8, near])
                    tr = m[0] - r * m[3]
                    ti = m[1] + r * m[2]
                    for slot, term in ((2 * k, cr * tr - ci * ti), (2 * k + 1, cr * ti + ci * tr)):
                        acc[slot] = term if acc[slot] is None else acc[slot] + term
                    if k + 1 < BAND:
                        pr, pi, cr, ci = cr, ci, twice * cr - pr, twice * ci - pi
            sums += acc
        for i in range(32):
            total[t, i] = total[t, i] + sums[i]

    ahead = BATCH // 128
    later = HALF // 128 - ahead
    lax.fori_loop(0, ahead, chunk, 0)
    for c in range(later):
        for part in range(PIECES * c // later, PIECES * (c + 1) // later):
            product(ready, 0, part)
        chunk(jnp.int32(ahead + c), 0)

    def step(i, carry):
        following = jnp.minimum(i + 1, steps - 1)

        @pl.when(lax.rem(i, 2) == 0)
        def _():
            consume(ready, i, after, following)

        @pl.when(lax.rem(i, 2) == 1)
        def _():
            consume(after, i, ready, following)

        return carry

    lax.fori_loop(0, steps, step, 0)

    lane_block = lax.broadcasted_iota(jnp.int32, (4, 128), 1) // 32
    for t in range(OBSERVERS // LIST):
        for lane in range(LIST // 128):
            sums = [jnp.sum(total[t, lane * 16 + i], axis=0, keepdims=True) for i in range(16)]
            packs = [
                jnp.concatenate(
                    [sums[2 * kk], sums[2 * kk + 1], sums[2 * (4 + kk)], sums[2 * (4 + kk) + 1]],
                    axis=0,
                )
                for kk in range(4)
            ]
            for m in range(4):
                value = None
                for kk in range(4):
                    shift = (32 * (kk - m)) % 128
                    turned = pltpu.roll(packs[kk], shift, axis=1) if shift else packs[kk]
                    value = turned if value is None else jnp.where(lane_block == kk, turned, value)
                for h in range(2):
                    out_ref[2 * (8 * t + 4 * lane + m) + h] = value[2 * h : 2 * h + 2]


def finish_kernel(parts_ref, out_ref):
    value = jnp.sum(parts_ref[...], axis=0)
    for kk in range(4):
        out_ref[:, kk, :] = value[:, 32 * kk : 32 * kk + 32]


def shape(*dims, dtype=F32):
    return jax.ShapeDtypeStruct(dims, dtype)


def on_device(series, panel_pos, panel_area, observers, owner):
    whole = pl.BlockSpec(memory_space=pltpu.VMEM)
    pack = jnp.concatenate(
        [
            panel_pos,
            panel_area,
            jnp.pad(observers, ((0, 0), (0, SLOTS - OBSERVERS))),
            owner.reshape(1, SLOTS).astype(F32),
        ],
        axis=0,
    )
    keep, send, begun = pl.pallas_call(
        source_kernel,
        out_shape=(shape(128, HALF), shape(128, HALF), shape(8, 128)),
        in_specs=[whole] * 2,
        out_specs=(whole,) * 3,
        compiler_params=params(),
        name="sources",
    )(jnp.transpose(series, (1, 0, 2)), pack)
    features = pl.pallas_call(
        feature_kernel,
        out_shape=shape(DEPTH, OBSERVERS, dtype=BF16),
        in_specs=[whole],
        out_specs=whole,
        compiler_params=params(),
        name="features",
    )(pack)
    swap = [(i, i ^ 1) for i in range(8)]
    above = [(i, (i + 2) % 8) for i in range(8)]
    below = [(i, (i + 6) % 8) for i in range(8)]
    recv = lax.ppermute(send, "obs", swap)

    pair_count = HALF * OBSERVERS
    early, ready = pl.pallas_call(
        early_kernel,
        out_shape=(shape(6, 128 * EARLY, OBSERVERS), shape(8, 128)),
        in_specs=[whole] * 2,
        out_specs=(whole, whole),
        scratch_shapes=[pltpu.VMEM((3, 128, 128), F32)],
        compiler_params=params(8),
        cost_estimate=pl.CostEstimate(
            flops=10 * pair_count, bytes_accessed=4 * MIB, transcendentals=0
        ),
        name="early",
    )(pack, begun)
    own, up, down, far, mark = pl.pallas_call(
        band_kernel,
        out_shape=(shape(16, 4 * HALF),) * 4 + (shape(8, 128),),
        in_specs=[whole] * 3,
        out_specs=(whole,) * 5,
        compiler_params=params(),
        name="bands",
    )(keep, recv, ready)

    geometry = pl.pallas_call(
        geometry_kernel,
        out_shape=shape(6, HALF, OBSERVERS),
        in_specs=[whole] * 3,
        out_specs=whole,
        scratch_shapes=[pltpu.VMEM((3, 128, 128), F32)],
        compiler_params=params(8),
        cost_estimate=pl.CostEstimate(
            flops=80 * pair_count, bytes_accessed=32 * MIB, transcendentals=0
        ),
        name="geometry",
    )(pack, mark, early)
    across = lax.ppermute(far, "obs", [(i, (i + 4) % 8) for i in range(8)])
    from_below = lax.ppermute(up, "obs", above)
    from_above = lax.ppermute(down, "obs", below)

    chunks = pl.pallas_call(
        field_kernel,
        out_shape=shape(64, 2, 128),
        in_specs=[whole] * 7,
        out_specs=whole,
        scratch_shapes=[
            pltpu.VMEM((512, 128), F32),
            pltpu.VMEM((HALF // GROUP, 32, GROUP, DEPTH), BF16),
            pltpu.VMEM((32 * BATCH, LIST), F32),
            pltpu.VMEM((32 * BATCH, LIST), F32),
            pltpu.VMEM((OBSERVERS // LIST, 32, 8, 128), F32),
        ],
        compiler_params=params(28),
        name="field",
    )(own, from_below, from_above, across, pack, features, geometry)

    members = [
        [8 * d + 2 * y + c for d in range(lax.axis_size("panel")) for c in range(2)]
        for y in range(CHIPS)
    ]
    parts = lax.all_to_all(
        chunks,
        ("panel", "obs"),
        split_axis=0,
        concat_axis=0,
        axis_index_groups=members,
        tiled=True,
    )
    value = pl.pallas_call(
        finish_kernel,
        out_shape=shape(2, 4, 32),
        in_specs=[whole],
        out_specs=whole,
        compiler_params=params(),
        name="finish",
    )(parts)
    return jnp.transpose(value, (2, 0, 1))


def solution(mesh):
    in_specs = (P("obs", None, "panel"), P(None, "panel"), P(None, "panel"), P(), P("panel"))
    out_specs = P("panel", None, "obs")
    return jax.shard_map(
        on_device, mesh=mesh, in_specs=in_specs, out_specs=out_specs, check_vma=False
    )
```

```python
import functools
import math

import jax
import jax.numpy as jnp
import numpy as np
from jax import lax
from jax.experimental import pallas as pl
from jax.experimental.pallas import tpu as pltpu
from jax.sharding import PartitionSpec as P

TIME = 256
FREQ = 32
MACH_NUMBER = 0.3
SAMPLE_SPACING = 0.04
FOUR_PI = 4.0 * math.pi
BASE = 2.0 * math.pi / (TIME * SAMPLE_SPACING)

OBSERVERS = 1024
SLOTS = 2048
HALF = SLOTS // 2
STEPS = 32
CHIPS = 4
BAND = 8
LIST = 256
GROUP = 16
BATCH = 256
PIECES = 16
EARLY = 1
DEPTH = 128
MIB = 1 << 20

F32 = jnp.float32
BF16 = jnp.bfloat16


def sine_fits():
    node = np.cos((np.arange(400) + 0.5) * np.pi / 400) * 0.5 + 0.5
    square = node * 0.66**2
    angle = np.sqrt(square)
    table = []
    for values, degree in ((np.sin(angle) / angle, 3), (np.cos(angle), 4)):
        fit = np.polynomial.chebyshev.Chebyshev.fit(square, values, degree, domain=[0, 0.66**2])
        table.append([float(v) for v in fit.convert(kind=np.polynomial.Polynomial).coef])
    return table


SIN_FIT, COS_FIT = sine_fits()


def fourier_rows():
    place = lax.axis_index("obs")
    chip, core = lax.div(place, 2), lax.rem(place, 2)
    row = lax.broadcasted_iota(jnp.int32, (64, 64), 0)
    lane = lax.broadcasted_iota(jnp.int32, (64, 64), 1)
    band = (chip + row // 16) & 3
    harmonic = BAND * band + (row & 7) + 1
    step = 64 * chip + ((lane + 32 * core) & 63)
    turns = (harmonic * step + 64 * ((row // 8) & 1)) & (TIME - 1)
    return jnp.cos(turns.astype(F32) * (2.0 * math.pi / TIME)) * (2.0 / TIME)


def params(mib=16):
    return pltpu.CompilerParams(vmem_limit_bytes=mib * MIB)


def split(value):
    high = value.astype(BF16)
    low = (value - high.astype(F32)).astype(BF16)
    return high, low


def source_kernel(series_ref, pack_ref, keep_ref, send_ref, mark_ref):
    mark_ref[...] = jnp.zeros(mark_ref.shape, F32)
    core = lax.rem(lax.axis_index("obs"), 2)
    area = pack_ref[3:6, :] * (pack_ref[9:10, :] >= 0).astype(F32)
    for pair in range(HALF // 128):
        blocks = []
        for side in range(2):
            lanes = slice(128 * (2 * pair + side), 128 * (2 * pair + side) + 128)
            field = [series_ref[f, :, lanes] for f in range(5)]
            b1, b2, b3 = area[0:1, lanes], area[1:2, lanes], area[2:3, lanes]
            bc = MACH_NUMBER * b1
            flux = b1 * field[1] + b2 * field[2] + b3 * field[3] + bc * field[0]
            blocks.append([flux] + [b * field[4] + bc * field[1 + i] for i, b in enumerate((b1, b2, b3))])
        lanes = slice(128 * pair, 128 * pair + 128)
        for f in range(4):
            even, odd = blocks[0][f], blocks[1][f]
            rows = slice(32 * f, 32 * f + 32)
            keep_ref[rows, lanes] = jnp.where(core == 0, even, odd)
            send_ref[rows, lanes] = jnp.where(core == 0, odd, even)


def feature_kernel(pack_ref, out_ref):
    x = pack_ref[6:9, 0:OBSERVERS]
    rows = jnp.concatenate(
        [
            jnp.ones((1, OBSERVERS), F32),
            x,
            x[0:1] * x[0:1] + x[1:2] * x[1:2] + x[2:3] * x[2:3],
        ],
        axis=0,
    )
    high = rows.astype(BF16).astype(F32)
    low = rows - high
    rest = jnp.zeros((1, OBSERVERS), F32)
    out_ref[...] = jnp.concatenate([high, high, low, rest] * BAND, axis=0).astype(BF16)


def band_kernel(keep_ref, recv_ref, given_ref, own_ref, up_ref, down_ref, far_ref, mark_ref):
    mark_ref[...] = given_ref[...]
    high, low = split(fourier_rows())
    table = jnp.concatenate([high, high, low], axis=1)
    for f in range(4):
        rows = slice(32 * f, 32 * f + 32)
        for tile in range(HALF // 256):
            lanes = slice(256 * tile, 256 * tile + 256)
            kh, kl = split(keep_ref[rows, lanes])
            rh, rl = split(recv_ref[rows, lanes])
            stack = jnp.concatenate([kh, rh, kl, rl, kh, rh], axis=0)
            part = jnp.dot(table, stack, preferred_element_type=F32)
            out = slice(HALF * f + 256 * tile, HALF * f + 256 * tile + 256)
            own_ref[:, out] = part[0:16]
            up_ref[:, out] = part[16:32]
            down_ref[:, out] = part[48:64]
            far_ref[:, out] = part[32:48]


def double(cosine, sine):
    twice = cosine + cosine
    return twice * cosine - 1.0, twice * sine


def early_kernel(pack_ref, mark_ref, geo_ref, done_ref, wide_ref):
    done_ref[...] = mark_ref[...]
    geometry_chunks(0, EARLY, pack_ref, geo_ref, wide_ref)


def geometry_kernel(pack_ref, mark_ref, early_ref, geo_ref, wide_ref):
    for i in range(6):
        geo_ref[i, 0 : 128 * EARLY, :] = early_ref[i]
    geometry_chunks(EARLY, HALF // 128, pack_ref, geo_ref, wide_ref)


def geometry_chunks(first_chunk, last_chunk, pack_ref, geo_ref, wide_ref):
    place = lax.axis_index("obs")
    core = lax.rem(place, 2)
    chip = lax.div(place, 2)

    def tile_step(power, first, t):
        lanes = pl.ds(pl.multiple_of(t * 128, 128), 128)
        x = [jnp.broadcast_to(pack_ref[6 + i : 7 + i, lanes], (8, 128)) for i in range(3)]
        for g in range(16):
            rows = pl.ds(pl.multiple_of(first + 8 * g, 8), 8)
            square = None
            for i in range(3):
                delta = x[i] - wide_ref[i, 8 * g : 8 * g + 8, :]
                square = delta * delta if square is None else square + delta * delta
            inverse = lax.rsqrt(square)
            r = square * inverse
            quarter = r * (0.25 * BASE) - 0.25 * math.pi
            s2 = quarter * quarter
            sine = s2 * SIN_FIT[-1] + SIN_FIT[-2]
            for c in SIN_FIT[-3::-1]:
                sine = sine * s2 + c
            sine = sine * quarter
            cosine = s2 * COS_FIT[-1] + COS_FIT[-2]
            for c in COS_FIT[-3::-1]:
                cosine = cosine * s2 + c
            cosine, sine = double(cosine, sine)
            twice = sine + sine
            er = twice * sine - 1.0
            ei = twice * cosine
            amp = inverse * inverse * (inverse * (1.0 / FOUR_PI))
            if power == 0:
                gr, gi = amp, jnp.zeros_like(amp)
            else:
                cr, ci = er, ei
                for _ in range(3):
                    cr, ci = double(cr, ci)
                if power == 2:
                    cr, ci = double(cr, ci)
                elif power == 3:
                    twice = cr + cr
                    fourth = twice * twice
                    cr, ci = cr * (fourth - 3.0), ci * (fourth - 1.0)
                gr, gi = amp * cr, amp * ci
            br, bi = (gr * er, gr * ei) if power == 0 else (gr * er - gi * ei, gr * ei + gi * er)
            for i, value in enumerate((r, er + er, gr, gi, br, bi)):
                geo_ref[i, rows, lanes] = value

    def body(power):
        def chunk(c, carry):
            wide = pl.multiple_of(c * 256, 256)
            pos = jnp.where(
                core == 0, pack_ref[0:3, pl.ds(wide, 128)], pack_ref[0:3, pl.ds(wide + 128, 128)]
            )
            pos = jnp.concatenate([pos, jnp.zeros((5, 128), F32)], axis=0)
            y = jnp.transpose(pos)
            for i in range(3):
                wide_ref[i] = jnp.broadcast_to(y[:, i : i + 1], (128, 128))

            def tile(t, inner):
                tile_step(power, c * 128, t)
                return inner

            lax.fori_loop(0, OBSERVERS // 128, tile, 0)
            return carry

        lax.fori_loop(first_chunk, last_chunk, chunk, 0)

    for power in range(CHIPS):
        pl.when(chip == power)(lambda power=power: body(power))


def build_left(spec, pack_ref, stage, left):
    core = lax.rem(lax.axis_index("obs"), 2)
    first_band = lax.div(lax.axis_index("obs"), 2) * BAND
    wave = (lax.broadcasted_iota(jnp.int32, (BAND, 128), 0) + (first_band + 1)).astype(F32) * BASE
    freq_of = lax.broadcasted_iota(jnp.int32, (128, 128), 1) // 16
    stage[...] = jnp.zeros(stage.shape, F32)

    def chunk(c, carry):
        wide = pl.multiple_of(c * 256, 256)
        y = jnp.where(
            core == 0, pack_ref[0:3, pl.ds(wide, 128)], pack_ref[0:3, pl.ds(wide + 128, 128)]
        )
        y = [y[i : i + 1] for i in range(3)]
        square = y[0] * y[0] + y[1] * y[1] + y[2] * y[2]
        flux = spec(0, c)
        load = [spec(1 + i, c) for i in range(3)]
        gains = (-wave * flux[1], wave * flux[0])
        moment = [
            -(y[0] * load[0][p] + y[1] * load[1][p] + y[2] * load[2][p]) for p in range(2)
        ]
        comps = []
        for p in range(2):
            g = gains[p]
            rows = [g * square + moment[p]]
            rows += [load[i][p] - 2.0 * (y[i] * g) for i in range(3)]
            comps.append(rows + [g])
        for p in range(2):
            comps.append([wave * moment[p]] + [wave * load[i][p] for i in range(3)])
        for comp, rows in enumerate(comps):
            for q, row in enumerate(rows):
                high = row.astype(BF16).astype(F32)
                for place, value in ((q, high), (5 + q, row - high), (10 + q, high)):
                    stage[pl.ds(128 * comp + place, 8, stride=16), :] = value
        for comp in range(4):
            turned = jnp.transpose(stage[128 * comp : 128 * comp + 128, :])
            for k in range(BAND):
                block = jnp.where(freq_of == k, turned, 0.0).astype(BF16)
                left[pl.ds(c * 8, 8), comp * BAND + k] = block.reshape(8, GROUP, DEPTH)
        return carry

    return chunk


def field_kernel(
    own_ref, up_ref, down_ref, far_ref, pack_ref, feature_ref,
    geo_ref,
    out_ref, stage, left, ready, after, total,
):
    def spec(f, c):
        lanes = pl.ds(pl.multiple_of(HALF * f + c * 128, 128), 128)
        value = own_ref[:, lanes] + up_ref[:, lanes] + (down_ref[:, lanes] + far_ref[:, lanes])
        return value[0:8], value[8:16]

    chunk = build_left(spec, pack_ref, stage, left)
    total[...] = jnp.zeros(total.shape, F32)
    batches = HALF // BATCH
    steps = batches * (OBSERVERS // LIST)
    groups = BATCH // GROUP

    def product(target, i, part):
        t, b = lax.div(i, batches), lax.rem(i, batches)
        size = 32 * GROUP * groups // PIECES
        if PIECES <= groups:
            lhs = left[pl.ds(b * groups + part * (groups // PIECES), groups // PIECES)]
        else:
            cut = PIECES // groups
            span = 32 // cut
            lhs = left[b * groups + part // cut, span * (part % cut) : span * (part % cut) + span]
        rhs = feature_ref[:, pl.ds(pl.multiple_of(t * LIST, LIST), LIST)]
        target[part * size : part * size + size] = jnp.dot(
            lhs.reshape(size, DEPTH), rhs, preferred_element_type=F32
        )

    def consume(source, i, target, following):
        t, b = lax.div(i, batches), lax.rem(i, batches)
        sums = []
        for lane in range(LIST // 128):
            lanes = pl.ds(pl.multiple_of(t * LIST + 128 * lane, 128), 128)
            near = slice(128 * lane, 128 * lane + 128)
            acc = [None] * 16
            for sub in range(BATCH // 8):
                piece, rest = divmod((lane * (BATCH // 8) + sub) * PIECES, BATCH // 4)
                if rest == 0:
                    product(target, following, piece)
                rows = pl.ds(pl.multiple_of(b * BATCH + 8 * sub, 8), 8)
                r, twice, pr, pi, cr, ci = [geo_ref[i, rows, lanes] for i in range(6)]
                for k in range(BAND):
                    m = []
                    for comp in range(4):
                        base = ((sub // 2) * 32 + comp * BAND + k) * GROUP + 8 * (sub % 2)
                        m.append(source[base : base + 8, near])
                    tr = m[0] - r * m[3]
                    ti = m[1] + r * m[2]
                    for slot, term in ((2 * k, cr * tr - ci * ti), (2 * k + 1, cr * ti + ci * tr)):
                        acc[slot] = term if acc[slot] is None else acc[slot] + term
                    if k + 1 < BAND:
                        pr, pi, cr, ci = cr, ci, twice * cr - pr, twice * ci - pi
            sums += acc
        for i in range(32):
            total[t, i] = total[t, i] + sums[i]

    ahead = BATCH // 128
    later = HALF // 128 - ahead
    lax.fori_loop(0, ahead, chunk, 0)
    for c in range(later):
        for part in range(PIECES * c // later, PIECES * (c + 1) // later):
            product(ready, 0, part)
        chunk(jnp.int32(ahead + c), 0)

    def step(i, carry):
        following = jnp.minimum(i + 1, steps - 1)

        @pl.when(lax.rem(i, 2) == 0)
        def _():
            consume(ready, i, after, following)

        @pl.when(lax.rem(i, 2) == 1)
        def _():
            consume(after, i, ready, following)

        return carry

    lax.fori_loop(0, steps, step, 0)

    lane_block = lax.broadcasted_iota(jnp.int32, (4, 128), 1) // 32
    for t in range(OBSERVERS // LIST):
        for lane in range(LIST // 128):
            sums = [jnp.sum(total[t, lane * 16 + i], axis=0, keepdims=True) for i in range(16)]
            packs = [
                jnp.concatenate(
                    [sums[2 * kk], sums[2 * kk + 1], sums[2 * (4 + kk)], sums[2 * (4 + kk) + 1]],
                    axis=0,
                )
                for kk in range(4)
            ]
            for m in range(4):
                value = None
                for kk in range(4):
                    shift = (32 * (kk - m)) % 128
                    turned = pltpu.roll(packs[kk], shift, axis=1) if shift else packs[kk]
                    value = turned if value is None else jnp.where(lane_block == kk, turned, value)
                for h in range(2):
                    out_ref[2 * (8 * t + 4 * lane + m) + h] = value[2 * h : 2 * h + 2]


def finish_kernel(parts_ref, out_ref):
    value = jnp.sum(parts_ref[...], axis=0)
    for kk in range(4):
        out_ref[:, kk, :] = value[:, 32 * kk : 32 * kk + 32]


def shape(*dims, dtype=F32):
    return jax.ShapeDtypeStruct(dims, dtype)


def on_device(series, panel_pos, panel_area, observers, owner):
    whole = pl.BlockSpec(memory_space=pltpu.VMEM)
    pack = jnp.concatenate(
        [
            panel_pos,
            panel_area,
            jnp.pad(observers, ((0, 0), (0, SLOTS - OBSERVERS))),
            owner.reshape(1, SLOTS).astype(F32),
        ],
        axis=0,
    )
    keep, send, begun = pl.pallas_call(
        source_kernel,
        out_shape=(shape(128, HALF), shape(128, HALF), shape(8, 128)),
        in_specs=[whole] * 2,
        out_specs=(whole,) * 3,
        compiler_params=params(),
        name="sources",
    )(jnp.transpose(series, (1, 0, 2)), pack)
    features = pl.pallas_call(
        feature_kernel,
        out_shape=shape(DEPTH, OBSERVERS, dtype=BF16),
        in_specs=[whole],
        out_specs=whole,
        compiler_params=params(),
        name="features",
    )(pack)
    swap = [(i, i ^ 1) for i in range(8)]
    above = [(i, (i + 2) % 8) for i in range(8)]
    below = [(i, (i + 6) % 8) for i in range(8)]
    recv = lax.ppermute(send, "obs", swap)

    pair_count = HALF * OBSERVERS
    early, ready = pl.pallas_call(
        early_kernel,
        out_shape=(shape(6, 128 * EARLY, OBSERVERS), shape(8, 128)),
        in_specs=[whole] * 2,
        out_specs=(whole, whole),
        scratch_shapes=[pltpu.VMEM((3, 128, 128), F32)],
        compiler_params=params(8),
        cost_estimate=pl.CostEstimate(
            flops=10 * pair_count, bytes_accessed=4 * MIB, transcendentals=0
        ),
        name="early",
    )(pack, begun)
    own, up, down, far, mark = pl.pallas_call(
        band_kernel,
        out_shape=(shape(16, 4 * HALF),) * 4 + (shape(8, 128),),
        in_specs=[whole] * 3,
        out_specs=(whole,) * 5,
        compiler_params=params(),
        name="bands",
    )(keep, recv, ready)

    geometry = pl.pallas_call(
        geometry_kernel,
        out_shape=shape(6, HALF, OBSERVERS),
        in_specs=[whole] * 3,
        out_specs=whole,
        scratch_shapes=[pltpu.VMEM((3, 128, 128), F32)],
        compiler_params=params(8),
        cost_estimate=pl.CostEstimate(
            flops=80 * pair_count, bytes_accessed=32 * MIB, transcendentals=0
        ),
        name="geometry",
    )(pack, mark, early)
    across = lax.ppermute(far, "obs", [(i, (i + 4) % 8) for i in range(8)])
    from_below = lax.ppermute(up, "obs", above)
    from_above = lax.ppermute(down, "obs", below)

    chunks = pl.pallas_call(
        field_kernel,
        out_shape=shape(64, 2, 128),
        in_specs=[whole] * 7,
        out_specs=whole,
        scratch_shapes=[
            pltpu.VMEM((512, 128), F32),
            pltpu.VMEM((HALF // GROUP, 32, GROUP, DEPTH), BF16),
            pltpu.VMEM((32 * BATCH, LIST), F32),
            pltpu.VMEM((32 * BATCH, LIST), F32),
            pltpu.VMEM((OBSERVERS // LIST, 32, 8, 128), F32),
        ],
        compiler_params=params(28),
        name="field",
    )(own, from_below, from_above, across, pack, features, geometry)

    members = [
        [8 * d + 2 * y + c for d in range(lax.axis_size("panel")) for c in range(2)]
        for y in range(CHIPS)
    ]
    parts = lax.all_to_all(
        chunks,
        ("panel", "obs"),
        split_axis=0,
        concat_axis=0,
        axis_index_groups=members,
        tiled=True,
    )
    value = pl.pallas_call(
        finish_kernel,
        out_shape=shape(2, 4, 32),
        in_specs=[whole],
        out_specs=whole,
        compiler_params=params(),
        name="finish",
    )(parts)
    return jnp.transpose(value, (2, 0, 1))


def solution(mesh):
    in_specs = (P("obs", None, "panel"), P(None, "panel"), P(None, "panel"), P(), P("panel"))
    out_specs = P("panel", None, "obs")
    return jax.shard_map(
        on_device, mesh=mesh, in_specs=in_specs, out_specs=out_specs, check_vma=False
    )
```
